256 devices in a mesh: rep: 4 (over z_hi), fsdp: 64 (over y, z_lo, x, core).
Axes of the slice: x: 4, y: 4, z: 8 (z_hi: 4, z_lo: 2; z = z_hi * 2 + z_lo), core: 2. Of those that a mesh axis runs over, the one named last changes fastest.
Arguments:
- tokens: bfloat16 [4, 16384, 9216], P('rep', 'fsdp'), may hold values from -16 to 16
- norm_gain: float32 [9216], replicated, may hold values from 0.1 to 1.9
- master_weight: float32 [4, 9216, 512], P('rep', 'fsdp'), may hold values from -0.0625 to 0.0625
- inner_moment: float32 [4, 9216, 512], P('rep', 'fsdp'), may hold values from -4 to 4
- inner_second: float32 [4, 9216, 512], P('rep', 'fsdp'), may hold values from 0.1 to 1
- cotangent: bfloat16 [4, 16384, 512], P('rep', 'fsdp'), may hold values from -0.125 to 0.125
- frag_global: float32 [2, 9216, 512], P(None, 'fsdp'), may hold values from -6 to 6
- frag_local: float32 [4, 2, 9216, 512], P('rep', None, 'fsdp'), may hold values from -6 to 6
- outer_momentum: float32 [2, 9216, 512], P(None, 'fsdp'), may hold values from -6 to 6
- fragment_index: int32 [1], replicated, may hold values from 0 to 511
Outputs:
- key_out: bfloat16 [4, 16384, 512], P('rep', 'fsdp')
- new_master: float32 [4, 9216, 512], P('rep', 'fsdp')
- new_moment: float32 [4, 9216, 512], P('rep', 'fsdp')
- new_second: float32 [4, 9216, 512], P('rep', 'fsdp')
- new_global: float32 [9216, 512], P('fsdp')
- new_outer: float32 [9216, 512], P('fsdp')
The draws below stay inside these ranges and needn't reach their ends.
All inputs are finite; a program needn't handle non-finite values.
Results may differ from the reference program's by a relative error of at most 0.0065.
Values may be sent and summed in bfloat16 or wider, within the bound.
A program may use at most 128 MiB of HBM per device.

```python
import math
import jax
import jax.numpy as jnp
from jax import lax

D = 9216
KW = 512
VW = 512
NFRAG = 2
TOKENS = 16384
N_REP = 4


def spiked(drawn, stream_key, source, target, parts, factor):
    def block_of(dim):
        return (jnp.arange(drawn.shape[dim]) // (drawn.shape[dim] // parts)).reshape((-1,) + (1,) * (drawn.ndim - 1 - dim))

    one_side = jax.random.permutation(stream_key, parts)[block_of(target)]
    far = (block_of(target) + parts // 2) % parts
    return jnp.where((block_of(source) == one_side) | (block_of(source) == far), factor * drawn, drawn)


def levels(rng, shape, shards, least, high):
    loudness, own = 1.0, jax.random.fold_in(rng, 6)
    for axis_at, shards_of in shards:
        heights = jnp.exp(jax.random.uniform(jax.random.fold_in(own, axis_at), (shards_of,), jnp.float32, least / len(shards), high / len(shards)))
        loudness = loudness * jnp.repeat(heights, shape[axis_at] // shards_of).reshape([-1 if axis == axis_at else 1 for axis in range(len(shape))])
    return loudness


def gaussian(own_key, extent, width, limit, shards=(), dtype=jnp.bfloat16):
    loudness = levels(own_key, extent, shards, -0.22, 0.18) if shards else 1.0
    array = jax.random.normal(own_key, extent, jnp.float32) * width * loudness
    return jnp.minimum(jnp.maximum(array, -limit), limit).astype(dtype)


def noise_with(rng, extent, spread, most, shards, heavy, dtype=jnp.bfloat16):
    result = spread * jax.random.normal(rng, extent, jnp.float32)
    if shards:
        result = result * levels(rng, extent, shards, -0.22, 0.18)
    return jnp.clip(spiked(result, jax.random.fold_in(rng, 3), *heavy), -most, most).astype(dtype)


def setup_inputs(seed: int = 0) -> dict:
    splits = jax.random.split(jax.random.key(seed), 11)
    return {
        "tokens": noise_with(splits[0], (N_REP, TOKENS, D), 1.0, 16.0, ((0, 4), (1, 64)), (1, 2, 64, 4.0)),
        "norm_gain": jnp.clip(1.0 + 0.18 * jax.random.normal(splits[1], (D,), jnp.float32), 0.1, 1.9),
        "master_weight": gaussian(splits[2], (N_REP, D, KW), D ** -0.5, 0.0625, ((0, 4), (1, 64)), jnp.float32),
        "inner_moment": gaussian(splits[3], (N_REP, D, KW), 0.3, 4.0, ((0, 4), (1, 64)), jnp.float32),
        "inner_second": jnp.clip(jnp.exp(math.log(1.0) - 2.3025851 * jax.random.uniform(splits[4], (N_REP, D, KW), jnp.float32) ** levels(splits[4], (N_REP, D, KW), ((0, 4), (1, 64)), -0.2, 0.2)), 0.1, 1.0),
        "cotangent": gaussian(splits[5], (N_REP, TOKENS, KW), (TOKENS ** -0.5), 0.125, ((0, 4), (1, 64))),
        "frag_global": gaussian(splits[6], (NFRAG, D, VW), 1.0, 6.0, ((1, 64),), jnp.float32),
        "frag_local": gaussian(splits[7], (N_REP, NFRAG, D, VW), 1.0, 6.0, ((0, 4), (2, 64)), jnp.float32),
        "outer_momentum": gaussian(splits[8], (NFRAG, D, VW), 0.5, 6.0, ((1, 64),), jnp.float32),
        "fragment_index": jax.random.randint(splits[9], (1,), 0, 256 * NFRAG).astype(jnp.int32),
    }


def inner_step(inputs, gain, master, moment, second, upstream):
    values = inputs.astype(jnp.float32)
    inverse_rms = lax.rsqrt(lax.optimization_barrier(jnp.mean(values * values, axis=-1, keepdims=True)) + 1e-05)
    normed = (values * inverse_rms * gain).astype(jnp.bfloat16)
    weight_bf = master.astype(jnp.bfloat16)
    key_rows = jnp.dot(normed, weight_bf, preferred_element_type=jnp.float32).astype(jnp.bfloat16)
    grad = jnp.dot(normed.T, upstream, preferred_element_type=jnp.float32)
    moment_next = 0.9 * moment + 0.1 * grad
    second_next = 0.95 * second + 0.05 * grad * grad
    master_next = master - 0.02 * (moment_next / (jnp.sqrt(second_next) + 1e-08) + 0.1 * master)
    return (key_rows, master_next, moment_next, second_next)

def reference(tokens, norm_gain, master_weight, inner_moment, inner_second, cotangent, frag_global, frag_local, outer_momentum, fragment_index):
    key_list, master_list, moment_list, second_list = ([], [], [], [])
    for replica in range(N_REP):
        outputs = inner_step(tokens[replica], norm_gain, master_weight[replica], inner_moment[replica], inner_second[replica], cotangent[replica])
        key_list.append(outputs[0])
        master_list.append(outputs[1])
        moment_list.append(outputs[2])
        second_list.append(outputs[3])
    outer_step = fragment_index[0].astype(jnp.int32)
    frag_pick = (outer_step % NFRAG).astype(jnp.int32)
    round_count = (outer_step // NFRAG).astype(jnp.float32)
    outer_rate = 0.7 * (1.0 - round_count / 512.0)
    frag_now = lax.dynamic_index_in_dim(frag_global, frag_pick, 0, keepdims=False)
    local_now = lax.dynamic_index_in_dim(frag_local, frag_pick, 1, keepdims=False)
    moment_now = lax.dynamic_index_in_dim(outer_momentum, frag_pick, 0, keepdims=False)
    pseudo_grad = lax.optimization_barrier(jnp.sum(frag_now[None] - local_now, axis=0)) / N_REP
    new_outer = 0.9 * moment_now + pseudo_grad
    new_global = frag_now - outer_rate * (pseudo_grad + 0.9 * new_outer)
    return (jnp.stack(key_list), jnp.stack(master_list), jnp.stack(moment_list), jnp.stack(second_list), new_global, new_outer)
```

```python
import functools

import jax
import jax.numpy as jnp
from jax import lax
from jax.experimental import pallas as pl
from jax.experimental.pallas import tpu as pltpu
from jax.sharding import PartitionSpec as P

MESH = pl.DeviceIdType.MESH
F32 = jnp.float32
BF16 = jnp.bfloat16
REPS = 4
SIDE = 4
PLANES = 2
STRIP = 32
N_SEMS = 160


def kernel(
    tokens_hbm, gain_hbm, master_hbm, cot_hbm, global_hbm, local_hbm, index_ref,
    key_ref, grad_ref, pseudo_ref,
    tok, gain, master, frag_now, frag_local, cot, cot_oth,
    w_own, w, norm, norm_oth, part, part_bf, e_in, s_in, s_sum, s_bf, e2_in, s2_in,
    t_sum, t_bf, z_in, key_own, key_oth, key_in, diffs,
    in_sem, send_sem, recv_sem,
):
    rows, cols = master.shape
    n_tok = tok.shape[0]
    half = cols // 2
    lo, hi = pl.ds(0, half), pl.ds(half, half)
    group = norm.shape[-1]
    pair = PLANES * rows

    me = lax.axis_index("fsdp")
    rep = lax.axis_index("rep")
    core = me % 2
    x = (me // 2) % SIDE
    z = (me // (2 * SIDE)) % PLANES
    y = me // (2 * SIDE * PLANES)
    home = core == z

    def dev(y_, z_, x_, c_):
        return {"fsdp": ((y_ * PLANES + z_) * SIDE + x_) * 2 + c_}

    def along(axis, step):
        if axis == "x":
            return dev(y, z, (x + step + SIDE) % SIDE, core)
        return dev((y + step + SIDE) % SIDE, z, x, core)

    count = [0]
    started = []

    def slot():
        count[0] += 1
        return count[0] - 1

    def push(src, dst, to, sem=None, recv=None):
        sem = slot() if sem is None else sem
        copy = pltpu.make_async_remote_copy(
            src_ref=src,
            dst_ref=dst,
            send_sem=send_sem.at[sem],
            recv_sem=recv_sem.at[sem if recv is None else recv],
            device_id=to,
            device_id_type=MESH,
        )
        copy.start()
        return copy

    def send(src, dst, to):
        copy = push(src, dst, to)
        started.append(copy)
        return copy

    loads = []

    def load(src, dst):
        copy = pltpu.make_async_copy(src, dst, in_sem.at[len(loads)])
        copy.start()
        loads.append(copy)
        return copy

    load_master = load(master_hbm, master)
    n_chunk = 4
    chunk = n_tok // n_chunk
    load_gain = load(gain_hbm, gain)
    load_tok = [load(tokens_hbm.at[pl.ds(i * chunk, chunk)], tok.at[pl.ds(i * chunk, chunk)]) for i in range(n_chunk)]
    load_cot = load(cot_hbm, cot)
    load_now = load(global_hbm, frag_now)
    load_loc = load(local_hbm, frag_local)

    barrier = pltpu.get_barrier_semaphore()
    other_core = dev(y, z, x, 1 - core)
    peers = [along("x", 1), along("x", -1), along("y", 1), along("y", -1), other_core,
             dev(y, 1 - z, x, core), dev(y, 1 - z, x, 1 - core)]
    peers += [{"rep": (rep + k) % REPS} for k in range(1, REPS)]
    for peer in peers:
        pl.semaphore_signal(barrier, inc=1, device_id=peer, device_id_type=MESH)

    load_master.wait()
    w_own[...] = master[...].astype(BF16)
    pl.semaphore_wait(barrier, len(peers))

    def w_rows(y_, x_, c_):
        return y_, pl.ds(pl.multiple_of(x_ * pair + c_ * rows, 16), rows)

    own_at = w.at[w_rows(y, x, core)]
    w_far, w_near = slot(), slot()
    w_got = (slot(), slot())
    far_copy = push(w_own, own_at, dev(y, 1 - z, x, z), w_far, w_got[0] + core)

    @pl.when(home)
    def _():
        w[w_rows(y, x, core)] = w_own[...]

    @pl.when(jnp.logical_not(home))
    def _():
        push(w_own, own_at, other_core, w_near, w_got[0] + core)

    load_cot.wait()
    cot_copy = send(cot, cot_oth, other_core)

    tiles = group // 128
    n_group = norm.shape[0] * norm.shape[1]
    width = n_group * group

    def normalise(i):
        load_tok[i].wait()

        @pl.loop(0, chunk // STRIP)
        def _(s):
            at = pl.ds(pl.multiple_of(i * chunk + s * STRIP, STRIP), STRIP)
            total = jnp.zeros((STRIP, 128), F32)
            for t in range(width // 128):
                v = tok[at, t * 128:(t + 1) * 128].astype(F32)
                total = total + v * v
            mean = jnp.sum(total, axis=-1, keepdims=True) / width
            inverse = lax.rsqrt(mean + 1e-05)
            for t in range(width // 128):
                g, l = t // tiles, t % tiles
                v = tok[at, t * 128:(t + 1) * 128].astype(F32)
                v = v * inverse * gain[:, t * 128:(t + 1) * 128]
                norm[g // PLANES, g % PLANES, at, l * 128:(l + 1) * 128] = v.astype(BF16)

    load_gain.wait()
    normalise(0)

    first, second = ("x", "y"), ("y", "x")
    at1, at2 = (x, y), (y, x)

    def block(hf, a, b):
        y_, x_ = (b, a) if hf == 0 else (a, b)
        return w_rows(y_ % SIDE, x_ % SIDE, hf)

    def cut(where, columns):
        return (*where, columns)

    STEP = (1, -1)
    SIDE_COLS = (lo, hi)
    for c_ in range(2):
        @pl.when(jnp.logical_not(jnp.logical_and(home, core == c_)))
        def _():
            pltpu.make_async_remote_copy(
                src_ref=w_own, dst_ref=own_at, send_sem=send_sem.at[w_far], recv_sem=recv_sem.at[w_got[c_]],
                device_id=other_core, device_id_type=MESH).wait_recv()

    def gather_second(hf, a):
        ref = w.at[block(hf, a, at2[hf])]
        return [send(ref, ref, along(second[hf], STEP[d])) for d in range(2)]

    def gather_forward(hf, copies, a):
        out = []
        for d in range(2):
            copies[d].wait_recv()
            ref = w.at[cut(block(hf, a, at2[hf] - STEP[d] + SIDE), SIDE_COLS[d])]
            out.append(send(ref, ref, along(second[hf], STEP[d])))
        return out

    one = []
    for hf in range(2):
        ref = w.at[block(hf, at1[hf], at2[hf])]
        one.append([send(ref, ref, along(first[hf], STEP[d])) for d in range(2)])
    two = [[gather_second(hf, at1[hf])] for hf in range(2)]

    for i in range(1, n_chunk):
        normalise(i)
    norm_copies = [send(norm.at[q, 1 - core], norm_oth.at[q], other_core) for q in range(SIDE)]

    load_now.wait()
    load_loc.wait()
    k = index_ref[0] % frag_now.shape[0]
    diffs[rep] = (frag_now[k] - frag_local[k]).astype(BF16)
    rep_copies = [send(diffs.at[rep], diffs.at[rep], {"rep": (rep + j) % REPS}) for j in range(1, REPS)]

    one_f = [[None, None], [None, None]]
    for hf in range(2):
        for d in range(2):
            one[hf][d].wait_recv()
            a = at1[hf] - STEP[d] + SIDE
            ref = w.at[cut(block(hf, a, at2[hf]), SIDE_COLS[d])]
            one_f[hf][d] = send(ref, ref, along(first[hf], STEP[d]))
            two[hf].append(gather_second(hf, a))

    piece = group // 3
    over_tokens = (((0,), (0,)), ((), ()))

    @pl.loop(0, SIDE)
    def _(q):
        for j in range(3):
            part[q, j * piece:(j + 1) * piece, :] = lax.dot_general(
                norm[q, core, :, j * piece:(j + 1) * piece], cot[...], over_tokens, preferred_element_type=F32)

    two_f = [[None] * SIDE, [None] * SIDE]
    for hf in range(2):
        two_f[hf][0] = gather_forward(hf, two[hf][0], at1[hf])
    for hf in range(2):
        for d in range(2):
            one_f[hf][d].wait_recv()
        two[hf].append(gather_second(hf, at1[hf] + 2))

    cot_copy.wait_recv()
    for copy in norm_copies:
        copy.wait_recv()

    @pl.loop(0, SIDE)
    def _(q):
        for j in range(3):
            total = part[q, j * piece:(j + 1) * piece, :] + lax.dot_general(
                norm_oth[q, :, j * piece:(j + 1) * piece], cot_oth[...], over_tokens, preferred_element_type=F32)
            part[q, j * piece:(j + 1) * piece, :] = total
            part_bf[q, j * piece:(j + 1) * piece, :] = total.astype(BF16)

    rel = (0, -1, 1, 2)
    for hf in range(2):
        for i in range(1, SIDE):
            two_f[hf][i] = gather_forward(hf, two[hf][i], at1[hf] + rel[i] + SIDE)

    order = (3, 2, 1, 0)
    e_copies = [[None] * SIDE, [None] * SIDE]
    d_copies = [[None] * SIDE, [None] * SIDE]
    for i in order:
        for hf in range(2):
            a = at1[hf] + rel[i] + SIDE
            e_copies[hf][i] = [
                send(part_bf.at[cut(block(hf, a, at2[hf] + 2), SIDE_COLS[d])], e_in.at[hf, d, i], along(second[hf], STEP[d]))
                for d in range(2)]
    for i in order:
        for hf in range(2):
            a = at1[hf] + rel[i] + SIDE
            d_copies[hf][i] = [
                send(part_bf.at[cut(block(hf, a, at2[hf] + STEP[d] + SIDE), SIDE_COLS[1 - d])],
                     s_in.at[hf, d, i, :, SIDE_COLS[1 - d]], along(second[hf], STEP[d]))
                for d in range(2)]

    for hf in range(2):
        for i in range(SIDE):
            for copy in two_f[hf][i]:
                copy.wait_recv()

    def keys(operand):
        total = jnp.dot(operand(0), w[0], preferred_element_type=F32)
        for q in range(1, SIDE):
            total = total + jnp.dot(operand(q), w[q], preferred_element_type=F32)
        return total

    key_oth[...] = keys(lambda q: norm_oth[q])
    key_copy = send(key_oth, key_in, other_core)

    c_copies = [[None] * SIDE, [None] * SIDE]

    def combine(i):
        for hf in range(2):
            a = at1[hf] + rel[i] + SIDE
            copies = []
            for d in range(2):
                e_copies[hf][i][d].wait_recv()
                where = cut(block(hf, a, at2[hf] + STEP[d] + SIDE), SIDE_COLS[d])
                part_bf[where] = (part[where] + e_in[hf, d, i].astype(F32)).astype(BF16)
                copies.append(send(part_bf.at[where], s_in.at[hf, d, i, :, SIDE_COLS[d]], along(second[hf], STEP[d])))
            c_copies[hf][i] = copies

    for i in order:
        combine(i)

    key_own[...] = keys(lambda q: norm[q, core])

    for copy in rep_copies:
        copy.wait_recv()
    pseudo_ref[...] = (
        diffs[0].astype(F32) + diffs[1].astype(F32) + diffs[2].astype(F32) + diffs[3].astype(F32)) / REPS

    key_copy.wait_recv()
    key_ref[...] = (key_own[...] + key_in[...]).astype(BF16)

    e2_copies = [None, None]
    d2_copies = [[None, None], [None, None]]
    for i in order:
        for hf in range(2):
            for d in range(2):
                c_copies[hf][i][d].wait_recv()
                d_copies[hf][i][d].wait_recv()
            a = at1[hf] + rel[i] + SIDE
            total = part[block(hf, a, at2[hf])] + s_in[hf, 0, i].astype(F32) + s_in[hf, 1, i].astype(F32)
            s_sum[hf, i] = total
            s_bf[hf, i] = total.astype(BF16)
            if i == 3:
                e2_copies[hf] = [
                    send(s_bf.at[hf, i, :, SIDE_COLS[d]], e2_in.at[hf, d], along(first[hf], STEP[d])) for d in range(2)]
            elif i > 0:
                d = 2 - i
                d2_copies[hf][d] = send(
                    s_bf.at[hf, i, :, SIDE_COLS[1 - d]], s2_in.at[hf, d, :, SIDE_COLS[1 - d]], along(first[hf], STEP[d]))

    c2_copies = [[None, None], [None, None]]
    for hf in range(2):
        for d in range(2):
            i = 2 - d
            e2_copies[hf][d].wait_recv()
            s_bf[hf, i, :, SIDE_COLS[d]] = (s_sum[hf, i, :, SIDE_COLS[d]] + e2_in[hf, d].astype(F32)).astype(BF16)
            c2_copies[hf][d] = send(
                s_bf.at[hf, i, :, SIDE_COLS[d]], s2_in.at[hf, d, :, SIDE_COLS[d]], along(first[hf], STEP[d]))
    for hf in range(2):
        for d in range(2):
            c2_copies[hf][d].wait_recv()
            d2_copies[hf][d].wait_recv()
        total = s_sum[hf, 0] + s2_in[hf, 0].astype(F32) + s2_in[hf, 1].astype(F32)
        t_sum[hf] = total
        t_bf[hf] = total.astype(BF16)

    z_near, z_far0, z_far1 = slot(), slot(), slot()
    z_got = (slot(), slot())

    @pl.when(home)
    def _():
        push(t_bf.at[1 - core], z_in.at[0], other_core, z_near, z_got[0])

    @pl.when(jnp.logical_not(home))
    def _():
        push(t_bf.at[0], z_in.at[1], dev(y, core, x, 0), z_far0, z_got[1])
        push(t_bf.at[1], z_in.at[1], dev(y, core, x, 1), z_far1, z_got[1])

    def z_copy(sem, got):
        return pltpu.make_async_remote_copy(
            src_ref=t_bf.at[0], dst_ref=z_in.at[0], send_sem=send_sem.at[sem], recv_sem=recv_sem.at[got],
            device_id=other_core, device_id_type=MESH)

    z_copy(z_far0, z_got[1]).wait_recv()

    @pl.when(home)
    def _():
        grad_ref[...] = t_sum[core] + z_in[1].astype(F32)

    @pl.when(jnp.logical_not(home))
    def _():
        z_copy(z_near, z_got[0]).wait_recv()
        grad_ref[...] = z_in[0].astype(F32) + z_in[1].astype(F32)

    far_copy.wait_send()

    @pl.when(home)
    def _():
        z_copy(z_near, z_got[0]).wait_send()

    @pl.when(jnp.logical_not(home))
    def _():
        z_copy(w_near, z_got[0]).wait_send()
        z_copy(z_far0, z_got[0]).wait_send()
        z_copy(z_far1, z_got[0]).wait_send()

    for copy in started:
        copy.wait_send()


def exchange(tokens, gain, master, cot, frag_global, frag_local, index):
    n_tok, width = tokens.shape
    rows, cols = master.shape
    n_group = SIDE * PLANES
    group = width // n_group
    half = cols // 2
    any_spec = pl.BlockSpec(memory_space=pl.ANY)
    vmem_spec = pl.BlockSpec(memory_space=pltpu.VMEM)
    return pl.pallas_call(
        kernel,
        out_shape=(
            jax.ShapeDtypeStruct((n_tok, cols), BF16),
            jax.ShapeDtypeStruct((rows, cols), F32),
            jax.ShapeDtypeStruct((rows, cols), F32),
        ),
        in_specs=[any_spec] * 6 + [pl.BlockSpec(memory_space=pltpu.SMEM)],
        out_specs=(vmem_spec,) * 3,
        scratch_shapes=[
            pltpu.VMEM((n_tok, width), BF16),
            pltpu.VMEM((1, width), F32),
            pltpu.VMEM((rows, cols), F32),
            pltpu.VMEM(frag_global.shape, F32),
            pltpu.VMEM(frag_local.shape, F32),
            pltpu.VMEM((n_tok, cols), BF16),
            pltpu.VMEM((n_tok, cols), BF16),
            pltpu.VMEM((rows, cols), BF16),
            pltpu.VMEM((SIDE, group, cols), BF16),
            pltpu.VMEM((SIDE, PLANES, n_tok, group), BF16),
            pltpu.VMEM((SIDE, n_tok, group), BF16),
            pltpu.VMEM((SIDE, group, cols), F32),
            pltpu.VMEM((SIDE, group, cols), BF16),
            pltpu.VMEM((2, 2, SIDE, rows, half), BF16),
            pltpu.VMEM((2, 2, SIDE, rows, cols), BF16),
            pltpu.VMEM((2, SIDE, rows, cols), F32),
            pltpu.VMEM((2, SIDE, rows, cols), BF16),
            pltpu.VMEM((2, 2, rows, half), BF16),
            pltpu.VMEM((2, 2, rows, cols), BF16),
            pltpu.VMEM((2, rows, cols), F32),
            pltpu.VMEM((2, rows, cols), BF16),
            pltpu.VMEM((2, rows, cols), BF16),
            pltpu.VMEM((n_tok, cols), F32),
            pltpu.VMEM((n_tok, cols), F32),
            pltpu.VMEM((n_tok, cols), F32),
            pltpu.VMEM((REPS, rows, cols), BF16),
            pltpu.SemaphoreType.DMA((12,)),
            pltpu.SemaphoreType.DMA((N_SEMS,)),
            pltpu.SemaphoreType.DMA((N_SEMS,)),
        ],
        compiler_params=pltpu.CompilerParams(
            collective_id=0, has_side_effects=True, vmem_limit_bytes=60 * 1024 * 1024
        ),
        cost_estimate=pl.CostEstimate(flops=4 * n_tok * width * cols, bytes_accessed=10 * 1024 * 1024, transcendentals=0),
    )(tokens, gain, master, cot, frag_global, frag_local, index)


def shards(
    tokens,
    norm_gain,
    master_weight,
    inner_moment,
    inner_second,
    cotangent,
    frag_global,
    frag_local,
    outer_momentum,
    fragment_index,
):
    master = master_weight[0]
    key_rows, grad, pseudo_grad = exchange(
        tokens[0], norm_gain[None], master, cotangent[0], frag_global, frag_local[0], fragment_index)
    moment_next = 0.9 * inner_moment[0] + 0.1 * grad
    second_next = 0.95 * inner_second[0] + 0.05 * grad * grad
    master_next = master - 0.02 * (moment_next / (jnp.sqrt(second_next) + 1e-08) + 0.1 * master)
    frag_total = frag_global.shape[0]
    outer_step = fragment_index[0]
    frag_pick = outer_step % frag_total
    round_count = (outer_step // frag_total).astype(jnp.float32)
    outer_rate = 0.7 * (1.0 - round_count / 512.0)
    frag_now = lax.dynamic_index_in_dim(frag_global, frag_pick, 0, keepdims=False)
    moment_now = lax.dynamic_index_in_dim(outer_momentum, frag_pick, 0, keepdims=False)
    new_outer = 0.9 * moment_now + pseudo_grad
    new_global = frag_now - outer_rate * (pseudo_grad + 0.9 * new_outer)
    return (
        key_rows[None],
        master_next[None],
        moment_next[None],
        second_next[None],
        new_global,
        new_outer,
    )


def solution(mesh):
    in_specs = (
        P("rep", "fsdp", None),
        P(),
        P("rep", "fsdp", None),
        P("rep", "fsdp", None),
        P("rep", "fsdp", None),
        P("rep", "fsdp", None),
        P(None, "fsdp", None),
        P("rep", None, "fsdp", None),
        P(None, "fsdp", None),
        P(),
    )
    out_specs = (
        P("rep", "fsdp", None),
        P("rep", "fsdp", None),
        P("rep", "fsdp", None),
        P("rep", "fsdp", None),
        P("fsdp", None),
        P("fsdp", None),
    )
    return jax.shard_map(shards, mesh=mesh, in_specs=in_specs, out_specs=out_specs, check_vma=False)
```

```python
import functools

import jax
import jax.numpy as jnp
from jax import lax
from jax.experimental import pallas as pl
from jax.experimental.pallas import tpu as pltpu
from jax.sharding import PartitionSpec as P

MESH = pl.DeviceIdType.MESH
F32 = jnp.float32
BF16 = jnp.bfloat16
REPS = 4
SIDE = 4
NFRAG = 2
PLANES = 2
STRIP = 32
N_SEMS = 192


def kernel(
    tokens_hbm, gain_hbm, master_hbm, cot_hbm, global_hbm, local_hbm, index_ref,
    key_ref, grad_ref, pseudo_ref,
    tok, gain, master, frag_now, frag_local, cot, cot_oth,
    w_own, w, norm, norm_oth, part, part_bf, e_in, s_in, s_sum, s_bf, e2_in, s2_in,
    t_sum, t_bf, z_in, key_own, key_oth, key_in, diffs, r_in, r_sum,
    in_sem, send_sem, recv_sem,
):
    rows, cols = master.shape
    n_tok = tok.shape[0]
    half = cols // 2
    lo, hi = pl.ds(0, half), pl.ds(half, half)
    group = norm.shape[-1]
    pair = PLANES * rows

    me = lax.axis_index("fsdp")
    rep = lax.axis_index("rep")
    core = me % 2
    x = (me // 2) % SIDE
    z = (me // (2 * SIDE)) % PLANES
    y = me // (2 * SIDE * PLANES)
    home = core == z

    def dev(y_, z_, x_, c_):
        return {"fsdp": ((y_ * PLANES + z_) * SIDE + x_) * 2 + c_}

    def along(axis, step):
        if axis == "x":
            return dev(y, z, (x + step + SIDE) % SIDE, core)
        return dev((y + step + SIDE) % SIDE, z, x, core)

    count = [0]
    started = []

    def slot():
        count[0] += 1
        return count[0] - 1

    def push(src, dst, to, sem=None, recv=None):
        sem = slot() if sem is None else sem
        copy = pltpu.make_async_remote_copy(
            src_ref=src,
            dst_ref=dst,
            send_sem=send_sem.at[sem],
            recv_sem=recv_sem.at[sem if recv is None else recv],
            device_id=to,
            device_id_type=MESH,
        )
        copy.start()
        return copy

    def send(src, dst, to):
        copy = push(src, dst, to)
        started.append(copy)
        return copy

    named = {}

    def remote(name, src, dst, to):
        if name not in named:
            named[name] = slot()
        return pltpu.make_async_remote_copy(
            src_ref=src, dst_ref=dst, send_sem=send_sem.at[named[name]], recv_sem=recv_sem.at[named[name]],
            device_id=to, device_id_type=MESH)

    loads = []

    def load(src, dst):
        copy = pltpu.make_async_copy(src, dst, in_sem.at[len(loads)])
        copy.start()
        loads.append(copy)
        return copy

    load_master = load(master_hbm, master)
    n_chunk = 4
    chunk = n_tok // n_chunk
    load_gain = load(gain_hbm, gain)
    load_tok = [load(tokens_hbm.at[pl.ds(i * chunk, chunk)], tok.at[pl.ds(i * chunk, chunk)]) for i in range(n_chunk)]
    load_cot = load(cot_hbm, cot)
    load_now = load(global_hbm, frag_now)
    load_loc = load(local_hbm, frag_local)

    barrier = pltpu.get_barrier_semaphore()
    other_core = dev(y, z, x, 1 - core)
    peers = [along("x", 1), along("x", -1), along("y", 1), along("y", -1), other_core,
             dev(y, 1 - z, x, core), dev(y, 1 - z, x, 1 - core)]
    peers += [{"rep": (rep + k) % REPS} for k in range(1, REPS)]
    for peer in peers:
        pl.semaphore_signal(barrier, inc=1, device_id=peer, device_id_type=MESH)

    load_master.wait()
    w_own[...] = master[...].astype(BF16)
    pl.semaphore_wait(barrier, len(peers))

    def w_rows(y_, x_, c_):
        return y_, pl.ds(pl.multiple_of(x_ * pair + c_ * rows, 16), rows)

    own_at = w.at[w_rows(y, x, core)]
    w_far, w_near = slot(), slot()
    w_got = (slot(), slot())
    far_copy = push(w_own, own_at, dev(y, 1 - z, x, z), w_far, w_got[0] + core)

    @pl.when(home)
    def _():
        w[w_rows(y, x, core)] = w_own[...]

    @pl.when(jnp.logical_not(home))
    def _():
        push(w_own, own_at, other_core, w_near, w_got[0] + core)

    load_cot.wait()
    cot_copy = send(cot, cot_oth, other_core)

    tiles = group // 128
    n_group = norm.shape[0] * norm.shape[1]
    width = n_group * group

    def normalise(i):
        load_tok[i].wait()

        @pl.loop(0, chunk // STRIP)
        def _(s):
            at = pl.ds(pl.multiple_of(i * chunk + s * STRIP, STRIP), STRIP)
            total = jnp.zeros((STRIP, 128), F32)
            for t in range(width // 128):
                v = tok[at, t * 128:(t + 1) * 128].astype(F32)
                total = total + v * v
            mean = jnp.sum(total, axis=-1, keepdims=True) / width
            inverse = lax.rsqrt(mean + 1e-05)
            for t in range(width // 128):
                g, l = t // tiles, t % tiles
                v = tok[at, t * 128:(t + 1) * 128].astype(F32)
                v = v * inverse * gain[:, t * 128:(t + 1) * 128]
                norm[g // PLANES, g % PLANES, at, l * 128:(l + 1) * 128] = v.astype(BF16)

    def swap(i):
        at = pl.ds(i * chunk, chunk)
        return send(norm.at[:, 1 - core, at], norm_oth.at[:, at], other_core)

    load_gain.wait()
    norm_copies = []
    for i in range(n_chunk - 1):
        normalise(i)
        norm_copies.append(swap(i))

    first, second = ("x", "y"), ("y", "x")
    at1, at2 = (x, y), (y, x)

    def block(hf, a, b):
        y_, x_ = (b, a) if hf == 0 else (a, b)
        return w_rows(y_ % SIDE, x_ % SIDE, hf)

    def cut(where, columns):
        return (*where, columns)

    STEP = (1, -1)
    SIDE_COLS = (lo, hi)
    for c_ in range(2):
        @pl.when(jnp.logical_not(jnp.logical_and(home, core == c_)))
        def _():
            pltpu.make_async_remote_copy(
                src_ref=w_own, dst_ref=own_at, send_sem=send_sem.at[w_far], recv_sem=recv_sem.at[w_got[c_]],
                device_id=other_core, device_id_type=MESH).wait_recv()

    rel = (0, -1, 1, 2)
    FULL = (pl.ds(0, cols), lo)
    SIDES = ((lo, hi), (pl.ds(0, half // 2), pl.ds(half // 2, half // 2)))

    def piece_of(hf, i, j, columns):
        return w.at[cut(block(hf, at1[hf] + rel[i] + SIDE, at2[hf] + rel[j] + SIDE), columns)]

    def g1(role, hf, d):
        ref = piece_of(hf, 0, 0, FULL[role])
        return remote((1, hf, d), ref, ref, along(first[hf], STEP[d]))

    def g1f(role, hf, d):
        ref = piece_of(hf, 1 + d, 0, SIDES[role][d])
        return remote((2, hf, d), ref, ref, along(first[hf], STEP[d]))

    def g2(role, hf, i, d):
        ref = piece_of(hf, i, 0, FULL[role])
        return remote((3, hf, i, d), ref, ref, along(second[hf], STEP[d]))

    def g2f(role, hf, i, d):
        ref = piece_of(hf, i, 1 + d, SIDES[role][d])
        return remote((4, hf, i, d), ref, ref, along(second[hf], STEP[d]))

    def gz(hf, i, j):
        ref = piece_of(hf, i, j, hi)
        return remote((5, hf, i, j), ref, ref, dev(y, 1 - z, x, core))

    def each_role(step):
        @pl.when(home)
        def _():
            step(0)

        @pl.when(jnp.logical_not(home))
        def _():
            step(1)

    def gather_start(role):
        for hf in range(2):
            for d in range(2):
                g1(role, hf, d).start()
        for hf in range(2):
            for d in range(2):
                g2(role, hf, 0, d).start()

    def gather_first(role):
        for hf in range(2):
            for d in range(2):
                g1(role, hf, d).wait_recv()
                g1f(role, hf, d).start()
                for d2 in range(2):
                    g2(role, hf, 1 + d, d2).start()
                if role == 0:
                    gz(hf, 1 + d, 0).start()

    def gather_turn(role):
        for hf in range(2):
            gather_on(role, hf, 0)
            for d in range(2):
                g1f(role, hf, d).wait_recv()
            for d in range(2):
                g2(role, hf, 3, d).start()
            if role == 0:
                gz(hf, 3, 0).start()

    def gather_on(role, hf, i):
        for d in range(2):
            g2(role, hf, i, d).wait_recv()
            g2f(role, hf, i, d).start()
            if role == 0:
                gz(hf, i, 1 + d).start()

    def gather_last(role, i):
        for hf in range(2):
            for d in range(2):
                g2f(role, hf, i, d).wait_recv()
            if role == 0:
                gz(hf, i, 3).start()

    def gather_all(role, done):
        for hf in range(2):
            for d in range(2):
                getattr(g1(role, hf, d), done)()
                getattr(g1f(role, hf, d), done)()
                for i in range(SIDE):
                    getattr(g2(role, hf, i, d), done)()
                    getattr(g2f(role, hf, i, d), done)()

    def gather_far(done):
        for hf in range(2):
            for i in range(SIDE):
                for j in range(SIDE):
                    if i or j:
                        getattr(gz(hf, i, j), done)()

    each_role(gather_start)

    normalise(n_chunk - 1)
    norm_copies.append(swap(n_chunk - 1))

    load_now.wait()
    load_loc.wait()
    k = index_ref[0] % frag_now.shape[0]
    diffs[...] = (frag_now[k] - frag_local[k]).astype(BF16)
    quarter = cols // REPS

    def quarter_of(r):
        return diffs.at[:, pl.ds(pl.multiple_of(r * quarter, quarter), quarter)]

    r_in[rep] = diffs[:, pl.ds(pl.multiple_of(rep * quarter, quarter), quarter)]
    rep_copies = [send(quarter_of((rep + j) % REPS), r_in.at[rep], {"rep": (rep + j) % REPS}) for j in range(1, REPS)]

    piece = group // 3
    over_tokens = (((0,), (0,)), ((), ()))

    @pl.loop(0, SIDE)
    def _(q):
        for j in range(3):
            part[q, j * piece:(j + 1) * piece, :] = lax.dot_general(
                norm[q, core, :, j * piece:(j + 1) * piece], cot[...], over_tokens, preferred_element_type=F32)

    each_role(gather_first)

    cot_copy.wait_recv()
    for copy in norm_copies:
        copy.wait_recv()

    @pl.loop(0, SIDE)
    def _(q):
        for j in range(3):
            total = part[q, j * piece:(j + 1) * piece, :] + lax.dot_general(
                norm_oth[q, :, j * piece:(j + 1) * piece], cot_oth[...], over_tokens, preferred_element_type=F32)
            part[q, j * piece:(j + 1) * piece, :] = total
            part_bf[q, j * piece:(j + 1) * piece, :] = total.astype(BF16)

    order = (3, 2, 1, 0)
    e_copies = [[None] * SIDE, [None] * SIDE]
    d_copies = [[None] * SIDE, [None] * SIDE]
    c_copies = [[None] * SIDE, [None] * SIDE]
    for i in order:
        for hf in range(2):
            a = at1[hf] + rel[i] + SIDE
            e_copies[hf][i] = [
                send(part_bf.at[cut(block(hf, a, at2[hf] + 2), SIDE_COLS[d])], e_in.at[hf, d, i], along(second[hf], STEP[d]))
                for d in range(2)]
    each_role(gather_turn)
    for i in order:
        for hf in range(2):
            a = at1[hf] + rel[i] + SIDE
            d_copies[hf][i] = [
                send(part_bf.at[cut(block(hf, a, at2[hf] + STEP[d] + SIDE), SIDE_COLS[1 - d])],
                     s_in.at[hf, d, i, :, SIDE_COLS[1 - d]], along(second[hf], STEP[d]))
                for d in range(2)]

    def combine(i):
        for hf in range(2):
            a = at1[hf] + rel[i] + SIDE
            copies = []
            for d in range(2):
                e_copies[hf][i][d].wait_recv()
                where = cut(block(hf, a, at2[hf] + STEP[d] + SIDE), SIDE_COLS[d])
                part_bf[where] = (part[where] + e_in[hf, d, i].astype(F32)).astype(BF16)
                copies.append(send(part_bf.at[where], s_in.at[hf, d, i, :, SIDE_COLS[d]], along(second[hf], STEP[d])))
            c_copies[hf][i] = copies

    e2_copies = [None, None]
    d2_copies = [[None, None], [None, None]]

    def settle(i):
        for hf in range(2):
            for d in range(2):
                d_copies[hf][i][d].wait_recv()
                c_copies[hf][i][d].wait_recv()
            a = at1[hf] + rel[i] + SIDE
            total = part[block(hf, a, at2[hf])] + s_in[hf, 0, i].astype(F32) + s_in[hf, 1, i].astype(F32)
            s_sum[hf, i] = total
            if i > 0:
                s_bf[hf, i] = total.astype(BF16)
            if i == 3:
                e2_copies[hf] = [
                    send(s_bf.at[hf, i, :, SIDE_COLS[d]], e2_in.at[hf, d], along(first[hf], STEP[d])) for d in range(2)]
            elif i > 0:
                d = 2 - i
                d2_copies[hf][d] = send(
                    s_bf.at[hf, i, :, SIDE_COLS[1 - d]], s2_in.at[hf, d, :, SIDE_COLS[1 - d]], along(first[hf], STEP[d]))

    def on(i):
        each_role(lambda role: [gather_on(role, hf, i) for hf in range(2)])

    def last(i):
        each_role(lambda role: gather_last(role, i))

    combine(3)
    combine(2)
    on(1)
    on(2)

    for copy in rep_copies:
        copy.wait_recv()
    r_sum[rep] = (r_in[0].astype(F32) + r_in[1].astype(F32) + r_in[2].astype(F32) + r_in[3].astype(F32)).astype(BF16)
    sum_copies = [send(r_sum.at[rep], r_sum.at[rep], {"rep": (rep + j) % REPS}) for j in range(1, REPS)]

    combine(1)
    settle(3)
    on(3)
    last(0)
    combine(0)
    last(1)
    last(2)
    settle(2)
    settle(1)

    c2_copies = [[None, None], [None, None]]
    for hf in range(2):
        for d in range(2):
            i = 2 - d
            e2_copies[hf][d].wait_recv()
            s_bf[hf, i, :, SIDE_COLS[d]] = (s_sum[hf, i, :, SIDE_COLS[d]] + e2_in[hf, d].astype(F32)).astype(BF16)
            c2_copies[hf][d] = send(
                s_bf.at[hf, i, :, SIDE_COLS[d]], s2_in.at[hf, d, :, SIDE_COLS[d]], along(first[hf], STEP[d]))

    last(3)

    settle(0)
    for hf in range(2):
        for d in range(2):
            c2_copies[hf][d].wait_recv()
            d2_copies[hf][d].wait_recv()
        total = s_sum[hf, 0] + s2_in[hf, 0].astype(F32) + s2_in[hf, 1].astype(F32)
        t_sum[hf] = total
        t_bf[hf] = total.astype(BF16)

    z_near, z_far0, z_far1 = slot(), slot(), slot()
    z_got = (slot(), slot())

    @pl.when(home)
    def _():
        push(t_bf.at[1 - core], z_in.at[0], other_core, z_near, z_got[0])

    @pl.when(jnp.logical_not(home))
    def _():
        push(t_bf.at[0], z_in.at[1], dev(y, core, x, 0), z_far0, z_got[1])
        push(t_bf.at[1], z_in.at[1], dev(y, core, x, 1), z_far1, z_got[1])

    @pl.when(jnp.logical_not(home))
    def _():
        gather_far("wait_recv")

    def keys(operand):
        total = jnp.dot(operand(0), w[0], preferred_element_type=F32)
        for q in range(1, SIDE):
            total = total + jnp.dot(operand(q), w[q], preferred_element_type=F32)
        return total

    key_oth[...] = keys(lambda q: norm_oth[q])
    key_copy = send(key_oth, key_in, other_core)
    key_own[...] = keys(lambda q: norm[q, core])
    key_copy.wait_recv()
    key_ref[...] = (key_own[...] + key_in[...]).astype(BF16)

    for copy in sum_copies:
        copy.wait_recv()
    for r in range(REPS):
        pseudo_ref[:, r * quarter:(r + 1) * quarter] = r_sum[r].astype(F32) / REPS

    def z_copy(sem, got):
        return pltpu.make_async_remote_copy(
            src_ref=t_bf.at[0], dst_ref=z_in.at[0], send_sem=send_sem.at[sem], recv_sem=recv_sem.at[got],
            device_id=other_core, device_id_type=MESH)

    z_copy(z_far0, z_got[1]).wait_recv()

    @pl.when(home)
    def _():
        grad_ref[...] = t_sum[core] + z_in[1].astype(F32)

    @pl.when(jnp.logical_not(home))
    def _():
        z_copy(z_near, z_got[0]).wait_recv()
        grad_ref[...] = z_in[0].astype(F32) + z_in[1].astype(F32)

    far_copy.wait_send()

    @pl.when(home)
    def _():
        z_copy(z_near, z_got[0]).wait_send()

    @pl.when(jnp.logical_not(home))
    def _():
        z_copy(w_near, z_got[0]).wait_send()
        z_copy(z_far0, z_got[0]).wait_send()
        z_copy(z_far1, z_got[0]).wait_send()

    each_role(lambda role: gather_all(role, "wait_send"))

    @pl.when(home)
    def _():
        gather_far("wait_send")

    for copy in started:
        copy.wait_send()


def exchange(tokens, gain, master, cot, frag_global, frag_local, index):
    n_tok, width = tokens.shape
    rows, cols = master.shape
    n_group = SIDE * PLANES
    group = width // n_group
    half = cols // 2
    any_spec = pl.BlockSpec(memory_space=pl.ANY)
    vmem_spec = pl.BlockSpec(memory_space=pltpu.VMEM)
    return pl.pallas_call(
        kernel,
        out_shape=(
            jax.ShapeDtypeStruct((n_tok, cols), BF16),
            jax.ShapeDtypeStruct((rows, cols), F32),
            jax.ShapeDtypeStruct((rows, cols), F32),
        ),
        in_specs=[any_spec] * 6 + [pl.BlockSpec(memory_space=pltpu.SMEM)],
        out_specs=(vmem_spec,) * 3,
        scratch_shapes=[
            pltpu.VMEM((n_tok, width), BF16),
            pltpu.VMEM((1, width), F32),
            pltpu.VMEM((rows, cols), F32),
            pltpu.VMEM(frag_global.shape, F32),
            pltpu.VMEM(frag_local.shape, F32),
            pltpu.VMEM((n_tok, cols), BF16),
            pltpu.VMEM((n_tok, cols), BF16),
            pltpu.VMEM((rows, cols), BF16),
            pltpu.VMEM((SIDE, group, cols), BF16),
            pltpu.VMEM((SIDE, PLANES, n_tok, group), BF16),
            pltpu.VMEM((SIDE, n_tok, group), BF16),
            pltpu.VMEM((SIDE, group, cols), F32),
            pltpu.VMEM((SIDE, group, cols), BF16),
            pltpu.VMEM((2, 2, SIDE, rows, half), BF16),
            pltpu.VMEM((2, 2, SIDE, rows, cols), BF16),
            pltpu.VMEM((2, SIDE, rows, cols), F32),
            pltpu.VMEM((2, SIDE, rows, cols), BF16),
            pltpu.VMEM((2, 2, rows, half), BF16),
            pltpu.VMEM((2, 2, rows, cols), BF16),
            pltpu.VMEM((2, rows, cols), F32),
            pltpu.VMEM((2, rows, cols), BF16),
            pltpu.VMEM((2, rows, cols), BF16),
            pltpu.VMEM((n_tok, cols), F32),
            pltpu.VMEM((n_tok, cols), F32),
            pltpu.VMEM((n_tok, cols), F32),
            pltpu.VMEM((rows, cols), BF16),
            pltpu.VMEM((REPS, rows, cols // REPS), BF16),
            pltpu.VMEM((REPS, rows, cols // REPS), BF16),
            pltpu.SemaphoreType.DMA((12,)),
            pltpu.SemaphoreType.DMA((N_SEMS,)),
            pltpu.SemaphoreType.DMA((N_SEMS,)),
        ],
        compiler_params=pltpu.CompilerParams(
            collective_id=0, has_side_effects=True, vmem_limit_bytes=60 * 1024 * 1024
        ),
        cost_estimate=pl.CostEstimate(flops=4 * n_tok * width * cols, bytes_accessed=10 * 1024 * 1024, transcendentals=0),
    )(tokens, gain, master, cot, frag_global, frag_local, index)


def update_kernel(
    index_ref, key_in, grad_in, pseudo_in, master, moment, second, frag_now, momentum,
    key_out, master_out, moment_out, second_out, global_out, outer_out,
):
    key_out[...] = key_in[...]
    grad = grad_in[...]
    moment_next = 0.9 * moment[...] + 0.1 * grad
    second_next = 0.95 * second[...] + 0.05 * grad * grad
    old = master[...]
    moment_out[...] = moment_next
    second_out[...] = second_next
    master_out[...] = old - 0.02 * (moment_next / (jnp.sqrt(second_next) + 1e-08) + 0.1 * old)
    round_count = (index_ref[0] // NFRAG).astype(F32)
    outer_rate = 0.7 * (1.0 - round_count / 512.0)
    pseudo = pseudo_in[...]
    new_outer = 0.9 * momentum[...] + pseudo
    outer_out[...] = new_outer
    global_out[...] = frag_now[...] - outer_rate * (pseudo + 0.9 * new_outer)


def update(index, key_rows, grad, pseudo, master, moment, second, frag_global, momentum):
    steps = 2
    rows, cols = grad.shape
    n_tok = key_rows.shape[0]
    key_spec = pl.BlockSpec((n_tok // steps, cols), lambda i, index: (i, 0))
    row_spec = pl.BlockSpec((rows // steps, cols), lambda i, index: (i, 0))
    frag_spec = pl.BlockSpec((None, rows // steps, cols), lambda i, index: (index[0] % NFRAG, i, 0))
    rows_f32 = jax.ShapeDtypeStruct((rows, cols), F32)
    return pl.pallas_call(
        update_kernel,
        out_shape=(jax.ShapeDtypeStruct(key_rows.shape, BF16),) + (rows_f32,) * 5,
        grid_spec=pltpu.PrefetchScalarGridSpec(
            num_scalar_prefetch=1,
            grid=(steps,),
            in_specs=[key_spec] + [row_spec] * 5 + [frag_spec] * 2,
            out_specs=(key_spec,) + (row_spec,) * 5,
        ),
    )(index, key_rows, grad, pseudo, master, moment, second, frag_global, momentum)


def shards(
    tokens,
    norm_gain,
    master_weight,
    inner_moment,
    inner_second,
    cotangent,
    frag_global,
    frag_local,
    outer_momentum,
    fragment_index,
):
    master = master_weight[0]
    key_rows, grad, pseudo_grad = exchange(
        tokens[0], norm_gain[None], master, cotangent[0], frag_global, frag_local[0], fragment_index)
    key_rows, master_next, moment_next, second_next, new_global, new_outer = update(
        fragment_index, key_rows, grad, pseudo_grad, master, inner_moment[0], inner_second[0], frag_global, outer_momentum)
    return (
        key_rows[None],
        master_next[None],
        moment_next[None],
        second_next[None],
        new_global,
        new_outer,
    )


def solution(mesh):
    in_specs = (
        P("rep", "fsdp", None),
        P(),
        P("rep", "fsdp", None),
        P("rep", "fsdp", None),
        P("rep", "fsdp", None),
        P("rep", "fsdp", None),
        P(None, "fsdp", None),
        P("rep", None, "fsdp", None),
        P(None, "fsdp", None),
        P(),
    )
    out_specs = (
        P("rep", "fsdp", None),
        P("rep", "fsdp", None),
        P("rep", "fsdp", None),
        P("rep", "fsdp", None),
        P("fsdp", None),
        P("fsdp", None),
    )
    return jax.shard_map(shards, mesh=mesh, in_specs=in_specs, out_specs=out_specs, check_vma=False)
```

```python
import functools

import jax
import jax.numpy as jnp
from jax import lax
from jax.experimental import pallas as pl
from jax.experimental.pallas import tpu as pltpu
from jax.sharding import PartitionSpec as P

MESH = pl.DeviceIdType.MESH
F32 = jnp.float32
BF16 = jnp.bfloat16
REPS = 4
SIDE = 4
NFRAG = 2
PLANES = 2
STRIP = 32
N_SEMS = 192


def kernel(
    tokens_hbm, gain_hbm, master_hbm, cot_hbm, global_hbm, local_hbm, moment_hbm, second_hbm, momentum_hbm, index_ref,
    key_ref, master_ref, moment_ref, second_ref, global_ref, outer_ref,
    tok, gain, master, old_moment, old_second, momentum, key_v, master_v, moment_v, second_v, global_v, outer_v, frag_now, frag_local, cot, cot_oth,
    w_own, w, norm, norm_oth, part, part_bf, e_in, s_in, s_sum, s_bf, e2_in, s2_in,
    t_sum, t_bf, z_in, key_own, key_oth, key_in, diffs, re_in, rs_in, r_sum,
    in_sem, out_sem, here_sem, send_sem, recv_sem,
):
    rows, cols = master.shape
    n_tok = tok.shape[0]
    half = cols // 2
    lo, hi = pl.ds(0, half), pl.ds(half, half)
    group = norm.shape[-1]
    pair = PLANES * rows

    me = lax.axis_index("fsdp")
    rep = lax.axis_index("rep")
    core = me % 2
    x = (me // 2) % SIDE
    z = (me // (2 * SIDE)) % PLANES
    y = me // (2 * SIDE * PLANES)
    home = core == z

    def dev(y_, z_, x_, c_):
        return {"fsdp": ((y_ * PLANES + z_) * SIDE + x_) * 2 + c_}

    def along(axis, step):
        if axis == "x":
            return dev(y, z, (x + step + SIDE) % SIDE, core)
        return dev((y + step + SIDE) % SIDE, z, x, core)

    count = [0]
    started = []

    def slot():
        count[0] += 1
        return count[0] - 1

    def push(src, dst, to, sem=None, recv=None):
        sem = slot() if sem is None else sem
        copy = pltpu.make_async_remote_copy(
            src_ref=src,
            dst_ref=dst,
            send_sem=send_sem.at[sem],
            recv_sem=recv_sem.at[sem if recv is None else recv],
            device_id=to,
            device_id_type=MESH,
        )
        copy.start()
        return copy

    def send(src, dst, to):
        copy = push(src, dst, to)
        started.append(copy)
        return copy

    named = {}

    def remote(name, src, dst, to):
        if name not in named:
            named[name] = slot()
        return pltpu.make_async_remote_copy(
            src_ref=src, dst_ref=dst, send_sem=send_sem.at[named[name]], recv_sem=recv_sem.at[named[name]],
            device_id=to, device_id_type=MESH)

    loads = []

    def load(src, dst):
        copy = pltpu.make_async_copy(src, dst, in_sem.at[len(loads)])
        copy.start()
        loads.append(copy)
        return copy

    load_master = load(master_hbm, master)
    n_chunk = 4
    chunk = n_tok // n_chunk
    load_gain = load(gain_hbm, gain)
    load_tok = [load(tokens_hbm.at[pl.ds(i * chunk, chunk)], tok.at[pl.ds(i * chunk, chunk)]) for i in range(n_chunk)]
    load_cot = load(cot_hbm, cot)
    load_now = load(global_hbm, frag_now)
    load_loc = load(local_hbm, frag_local)
    load_rest = [load(moment_hbm, old_moment), load(second_hbm, old_second), load(momentum_hbm, momentum)]
    stores = []

    def store(src, dst):
        copy = pltpu.make_async_copy(src, dst, out_sem.at[len(stores)])
        copy.start()
        stores.append(copy)


    barrier = pltpu.get_barrier_semaphore()
    other_core = dev(y, z, x, 1 - core)
    peers = [along("x", 1), along("x", -1), along("y", 1), along("y", -1), other_core,
             dev(y, 1 - z, x, core), dev(y, 1 - z, x, 1 - core)]
    for peer in peers:
        pl.semaphore_signal(barrier, inc=1, device_id=peer, device_id_type=MESH)

    def rep_at(step):
        return {"rep": (rep + step + REPS) % REPS}

    STEP = (1, -1)
    for step in STEP:
        @pl.when(rep < (rep + step + REPS) % REPS)
        def _():
            pl.semaphore_signal(barrier, inc=1, device_id=rep_at(step), device_id_type=MESH)

    lower = (rep + 1) // 2

    load_master.wait()
    w_own[...] = master[...].astype(BF16)
    pl.semaphore_wait(barrier, len(peers) + lower)
    for step in STEP:
        @pl.when(rep > (rep + step + REPS) % REPS)
        def _():
            pl.semaphore_signal(here_sem, inc=1, device_id=rep_at(step), device_id_type=MESH)

    def w_rows(y_, x_, c_):
        return y_, pl.ds(pl.multiple_of(x_ * pair + c_ * rows, 16), rows)

    own_at = w.at[w_rows(y, x, core)]
    w_far, w_near = slot(), slot()
    w_got = (slot(), slot())
    far_copy = push(w_own, own_at, dev(y, 1 - z, x, z), w_far, w_got[0] + core)

    @pl.when(home)
    def _():
        w[w_rows(y, x, core)] = w_own[...]

    @pl.when(jnp.logical_not(home))
    def _():
        push(w_own, own_at, other_core, w_near, w_got[0] + core)

    tiles = group // 128
    n_group = norm.shape[0] * norm.shape[1]
    width = n_group * group

    def normalise(i):
        load_tok[i].wait()

        @pl.loop(0, chunk // STRIP)
        def _(s):
            at = pl.ds(pl.multiple_of(i * chunk + s * STRIP, STRIP), STRIP)
            total = jnp.zeros((STRIP, 128), F32)
            for t in range(width // 128):
                v = tok[at, t * 128:(t + 1) * 128].astype(F32)
                total = total + v * v
            mean = jnp.sum(total, axis=-1, keepdims=True) / width
            inverse = lax.rsqrt(mean + 1e-05)
            for t in range(width // 128):
                g, l = t // tiles, t % tiles
                v = tok[at, t * 128:(t + 1) * 128].astype(F32)
                v = v * inverse * gain[:, t * 128:(t + 1) * 128]
                norm[g // PLANES, g % PLANES, at, l * 128:(l + 1) * 128] = v.astype(BF16)

    def swap(i):
        at = pl.ds(i * chunk, chunk)
        return send(norm.at[:, 1 - core, at], norm_oth.at[:, at], other_core)

    first, second = ("x", "y"), ("y", "x")
    at1, at2 = (x, y), (y, x)

    def block(hf, a, b):
        y_, x_ = (b, a) if hf == 0 else (a, b)
        return w_rows(y_ % SIDE, x_ % SIDE, hf)

    def cut(where, columns):
        return (*where, columns)

    SIDE_COLS = (lo, hi)
    rel = (0, -1, 1, 2)
    FULL = (pl.ds(0, cols), lo)
    SIDES = ((lo, hi), (pl.ds(0, half // 2), pl.ds(half // 2, half // 2)))

    def piece_of(hf, i, j, columns):
        return w.at[cut(block(hf, at1[hf] + rel[i] + SIDE, at2[hf] + rel[j] + SIDE), columns)]

    def g1(role, hf, d):
        ref = piece_of(hf, 0, 0, FULL[role])
        return remote((1, hf, d), ref, ref, along(first[hf], STEP[d]))

    def g1f(role, hf, d):
        ref = piece_of(hf, 1 + d, 0, SIDES[role][d])
        return remote((2, hf, d), ref, ref, along(first[hf], STEP[d]))

    def g2(role, hf, i, d):
        ref = piece_of(hf, i, 0, FULL[role])
        return remote((3, hf, i, d), ref, ref, along(second[hf], STEP[d]))

    def g2f(role, hf, i, d):
        ref = piece_of(hf, i, 1 + d, SIDES[role][d])
        return remote((4, hf, i, d), ref, ref, along(second[hf], STEP[d]))

    def gz(hf, i, j):
        ref = piece_of(hf, i, j, hi)
        return remote((5, hf, i, j), ref, ref, dev(y, 1 - z, x, core))

    def each_role(step):
        @pl.when(home)
        def _():
            step(0)

        @pl.when(jnp.logical_not(home))
        def _():
            step(1)

    def gather_start(role):
        for hf in range(2):
            for d in range(2):
                g1(role, hf, d).start()
        for hf in range(2):
            for d in range(2):
                g2(role, hf, 0, d).start()

    def gather_first(role):
        for hf in range(2):
            for d in range(2):
                g1(role, hf, d).wait_recv()
                g1f(role, hf, d).start()
                for d2 in range(2):
                    g2(role, hf, 1 + d, d2).start()
                if role == 0:
                    gz(hf, 1 + d, 0).start()

    def gather_turn(role):
        for hf in range(2):
            gather_on(role, hf, 0)
            for d in range(2):
                g1f(role, hf, d).wait_recv()
            for d in range(2):
                g2(role, hf, 3, d).start()
            if role == 0:
                gz(hf, 3, 0).start()

    def gather_on(role, hf, i):
        for d in range(2):
            g2(role, hf, i, d).wait_recv()
            g2f(role, hf, i, d).start()
            if role == 0:
                gz(hf, i, 1 + d).start()

    def gather_last(role, i):
        for hf in range(2):
            for d in range(2):
                g2f(role, hf, i, d).wait_recv()
            if role == 0:
                gz(hf, i, 3).start()

    def gather_all(role, done):
        for hf in range(2):
            for d in range(2):
                getattr(g1(role, hf, d), done)()
                getattr(g1f(role, hf, d), done)()
                for i in range(SIDE):
                    getattr(g2(role, hf, i, d), done)()
                    getattr(g2f(role, hf, i, d), done)()

    def gather_far(done):
        for hf in range(2):
            for i in range(SIDE):
                for j in range(SIDE):
                    if i or j:
                        getattr(gz(hf, i, j), done)()

    def w_wait(c_):
        pltpu.make_async_remote_copy(
            src_ref=w_own, dst_ref=own_at, send_sem=send_sem.at[w_far], recv_sem=recv_sem.at[w_got[c_]],
            device_id=other_core, device_id_type=MESH).wait_recv()

    @pl.when(home)
    def _():
        for c_ in range(2):
            @pl.when(core != c_)
            def _():
                w_wait(c_)
        gather_start(0)

    load_cot.wait()
    cot_copy = send(cot, cot_oth, other_core)

    load_gain.wait()
    norm_copies = []
    for i in range(2):
        normalise(i)
        norm_copies.append(swap(i))

    @pl.when(jnp.logical_not(home))
    def _():
        for c_ in range(2):
            w_wait(c_)
        gather_start(1)

    for i in range(2, n_chunk):
        normalise(i)
        norm_copies.append(swap(i))

    load_now.wait()
    load_loc.wait()
    for copy in load_rest:
        copy.wait()
    k = index_ref[0] % frag_now.shape[0]
    diffs[...] = frag_now[k] - frag_local[k]
    quarter = cols // REPS
    ROWS = (pl.ds(0, rows // 2), pl.ds(rows // 2, rows // 2))

    def quarter_of(step, where):
        r = (rep + step + REPS) % REPS
        return where, pl.ds(pl.multiple_of(r * quarter, quarter), quarter)

    def r_e(d):
        return remote((6, d), diffs.at[quarter_of(2, ROWS[d])], re_in.at[d], rep_at(STEP[d]))

    def r_d(d):
        return remote((7, d), diffs.at[quarter_of(STEP[d], ROWS[1 - d])], rs_in.at[d, ROWS[1 - d]], rep_at(STEP[d]))

    def r_c(d):
        return remote((8, d), diffs.at[quarter_of(STEP[d], ROWS[d])], rs_in.at[d, ROWS[d]], rep_at(STEP[d]))

    def r_g(d):
        return remote((9, d), r_sum.at[rep], r_sum.at[rep], rep_at(STEP[d]))

    def r_f(d):
        ref = r_sum.at[(rep - STEP[d] + REPS) % REPS, ROWS[d]]
        return remote((10, d), ref, ref, rep_at(STEP[d]))

    def rep_start():
        @pl.when(lower < 2)
        def _():
            pl.semaphore_wait(here_sem, 2 - lower)

        for d in range(2):
            r_e(d).start()
        for d in range(2):
            r_d(d).start()

    def rep_combine():
        for d in range(2):
            r_e(d).wait_recv()
            where = quarter_of(STEP[d], ROWS[d])
            diffs[where] = diffs[where] + re_in[d]
            r_c(d).start()

    def rep_sum():
        for d in range(2):
            r_d(d).wait_recv()
            r_c(d).wait_recv()
        r_sum[rep] = diffs[quarter_of(0, pl.ds(0, rows))] + rs_in[0] + rs_in[1]
        for d in range(2):
            r_g(d).start()

    def rep_forward():
        for d in range(2):
            r_g(d).wait_recv()
            r_f(d).start()

    def rep_end():
        for d in range(2):
            r_f(d).wait_recv()
        round_count = (index_ref[0] // NFRAG).astype(F32)
        outer_rate = 0.7 * (1.0 - round_count / 512.0)
        for r in range(REPS):
            at = pl.ds(r * quarter, quarter)
            pseudo = r_sum[r] / REPS
            outer = 0.9 * momentum[k, :, at] + pseudo
            outer_v[:, at] = outer
            global_v[:, at] = frag_now[k, :, at] - outer_rate * (pseudo + 0.9 * outer)
        store(outer_v, outer_ref)
        store(global_v, global_ref)

    piece = group // 3
    over_tokens = (((0,), (0,)), ((), ()))

    @pl.loop(0, SIDE)
    def _(q):
        for j in range(3):
            part[q, j * piece:(j + 1) * piece, :] = lax.dot_general(
                norm[q, core, :, j * piece:(j + 1) * piece], cot[...], over_tokens, preferred_element_type=F32)

    each_role(gather_first)
    cot_copy.wait_recv()
    for copy in norm_copies:
        copy.wait_recv()

    @pl.loop(0, SIDE)
    def _(q):
        for j in range(3):
            total = part[q, j * piece:(j + 1) * piece, :] + lax.dot_general(
                norm_oth[q, :, j * piece:(j + 1) * piece], cot_oth[...], over_tokens, preferred_element_type=F32)
            part[q, j * piece:(j + 1) * piece, :] = total
            part_bf[q, j * piece:(j + 1) * piece, :] = total.astype(BF16)

    order = (3, 2, 1, 0)
    e_copies = [[None] * SIDE, [None] * SIDE]
    d_copies = [[None] * SIDE, [None] * SIDE]
    c_copies = [[None] * SIDE, [None] * SIDE]
    def spread(i):
        for hf in range(2):
            a = at1[hf] + rel[i] + SIDE
            e_copies[hf][i] = [
                send(part_bf.at[cut(block(hf, a, at2[hf] + 2), SIDE_COLS[d])], e_in.at[hf, d, i], along(second[hf], STEP[d]))
                for d in range(2)]

    def direct(i):
        for hf in range(2):
            a = at1[hf] + rel[i] + SIDE
            d_copies[hf][i] = [
                send(part_bf.at[cut(block(hf, a, at2[hf] + STEP[d] + SIDE), SIDE_COLS[1 - d])],
                     s_in.at[hf, d, i, :, SIDE_COLS[1 - d]], along(second[hf], STEP[d]))
                for d in range(2)]

    def combine(i):
        for hf in range(2):
            a = at1[hf] + rel[i] + SIDE
            copies = []
            for d in range(2):
                e_copies[hf][i][d].wait_recv()
                where = cut(block(hf, a, at2[hf] + STEP[d] + SIDE), SIDE_COLS[d])
                part_bf[where] = (part[where] + e_in[hf, d, i].astype(F32)).astype(BF16)
                copies.append(send(part_bf.at[where], s_in.at[hf, d, i, :, SIDE_COLS[d]], along(second[hf], STEP[d])))
            c_copies[hf][i] = copies

    e2_copies = [None, None]
    d2_copies = [[None, None], [None, None]]

    def settle(i):
        for hf in range(2):
            for d in range(2):
                d_copies[hf][i][d].wait_recv()
                c_copies[hf][i][d].wait_recv()
            a = at1[hf] + rel[i] + SIDE
            total = part[block(hf, a, at2[hf])] + s_in[hf, 0, i].astype(F32) + s_in[hf, 1, i].astype(F32)
            s_sum[hf, i] = total
            if i > 0:
                s_bf[hf, i] = total.astype(BF16)
            if i == 3:
                e2_copies[hf] = [
                    send(s_bf.at[hf, i, :, SIDE_COLS[d]], e2_in.at[hf, d], along(first[hf], STEP[d])) for d in range(2)]
            elif i > 0:
                d = 2 - i
                d2_copies[hf][d] = send(
                    s_bf.at[hf, i, :, SIDE_COLS[1 - d]], s2_in.at[hf, d, :, SIDE_COLS[1 - d]], along(first[hf], STEP[d]))

    c2_copies = [[None, None], [None, None]]

    def cross():
        for hf in range(2):
            for d in range(2):
                i = 2 - d
                e2_copies[hf][d].wait_recv()
                s_bf[hf, i, :, SIDE_COLS[d]] = (s_sum[hf, i, :, SIDE_COLS[d]] + e2_in[hf, d].astype(F32)).astype(BF16)
                c2_copies[hf][d] = send(
                    s_bf.at[hf, i, :, SIDE_COLS[d]], s2_in.at[hf, d, :, SIDE_COLS[d]], along(first[hf], STEP[d]))

    def on(i):
        each_role(lambda role: [gather_on(role, hf, i) for hf in range(2)])

    def last(i):
        each_role(lambda role: gather_last(role, i))

    spread(3)
    spread(2)
    spread(1)
    spread(0)
    each_role(gather_turn)
    rep_start()
    combine(3)
    direct(3)
    combine(2)
    direct(2)
    on(1)
    on(2)
    rep_combine()
    combine(1)
    direct(1)
    settle(3)
    on(3)
    last(0)
    combine(0)
    direct(0)
    rep_sum()
    last(1)
    last(2)
    settle(2)
    settle(1)
    rep_forward()
    cross()
    last(3)
    settle(0)
    for hf in range(2):
        for d in range(2):
            c2_copies[hf][d].wait_recv()
            d2_copies[hf][d].wait_recv()
        total = s_sum[hf, 0] + s2_in[hf, 0].astype(F32) + s2_in[hf, 1].astype(F32)
        t_sum[hf] = total
        t_bf[hf] = total.astype(BF16)

    z_near, z_far0, z_far1 = slot(), slot(), slot()
    z_got = (slot(), slot())

    @pl.when(home)
    def _():
        push(t_bf.at[1 - core], z_in.at[0], other_core, z_near, z_got[0])

    @pl.when(jnp.logical_not(home))
    def _():
        push(t_bf.at[0], z_in.at[1], dev(y, core, x, 0), z_far0, z_got[1])
        push(t_bf.at[1], z_in.at[1], dev(y, core, x, 1), z_far1, z_got[1])

    def in_last(hf, i, j):
        return (j if hf == 0 else i) == 3

    def far_wait(late):
        @pl.when(jnp.logical_not(home))
        def _():
            for hf in range(2):
                for i in range(SIDE):
                    for j in range(SIDE):
                        if (i or j) and in_last(hf, i, j) == late:
                            gz(hf, i, j).wait_recv()

    def key_terms(operand, steps):
        total = None
        for step in steps:
            q = (y + step) % SIDE
            term = jnp.dot(operand(q), w[q], preferred_element_type=F32)
            total = term if total is None else total + term
        return total

    far_wait(False)
    key_oth[...] = key_terms(lambda q: norm_oth[q], (0, 1, 3))
    key_own[...] = key_terms(lambda q: norm[q, core], (0, 1, 3))
    far_wait(True)
    key_oth[...] = key_oth[...] + key_terms(lambda q: norm_oth[q], (2,))
    key_copy = send(key_oth, key_in, other_core)
    key_own[...] = key_own[...] + key_terms(lambda q: norm[q, core], (2,))
    rep_end()
    key_copy.wait_recv()
    key_v[...] = (key_own[...] + key_in[...]).astype(BF16)
    store(key_v, key_ref)

    def z_copy(sem, got):
        return pltpu.make_async_remote_copy(
            src_ref=t_bf.at[0], dst_ref=z_in.at[0], send_sem=send_sem.at[sem], recv_sem=recv_sem.at[got],
            device_id=other_core, device_id_type=MESH)

    z_copy(z_far0, z_got[1]).wait_recv()

    def step_with(near):
        grad = near + z_in[1].astype(F32)
        old = master[...]
        moment_next = 0.9 * old_moment[...] + 0.1 * grad
        second_next = 0.95 * old_second[...] + 0.05 * grad * grad
        moment_v[...] = moment_next
        second_v[...] = second_next
        master_v[...] = old - 0.02 * (moment_next / (jnp.sqrt(second_next) + 1e-08) + 0.1 * old)

    @pl.when(home)
    def _():
        step_with(t_sum[core])

    @pl.when(jnp.logical_not(home))
    def _():
        z_copy(z_near, z_got[0]).wait_recv()
        step_with(z_in[0].astype(F32))

    store(master_v, master_ref)
    store(moment_v, moment_ref)
    store(second_v, second_ref)

    far_copy.wait_send()

    @pl.when(home)
    def _():
        z_copy(z_near, z_got[0]).wait_send()

    @pl.when(jnp.logical_not(home))
    def _():
        z_copy(w_near, z_got[0]).wait_send()
        z_copy(z_far0, z_got[0]).wait_send()
        z_copy(z_far1, z_got[0]).wait_send()

    each_role(lambda role: gather_all(role, "wait_send"))

    @pl.when(home)
    def _():
        gather_far("wait_send")

    for d in range(2):
        for copy in (r_e(d), r_d(d), r_c(d), r_g(d), r_f(d)):
            copy.wait_send()

    for copy in started:
        copy.wait_send()
    for copy in stores:
        copy.wait()


def exchange(tokens, gain, master, cot, frag_global, frag_local, moment, second, momentum, index):
    n_tok, width = tokens.shape
    rows, cols = master.shape
    n_group = SIDE * PLANES
    group = width // n_group
    half = cols // 2
    any_spec = pl.BlockSpec(memory_space=pl.ANY)
    rows_f32 = jax.ShapeDtypeStruct((rows, cols), F32)
    return pl.pallas_call(
        kernel,
        out_shape=(jax.ShapeDtypeStruct((n_tok, cols), BF16),) + (rows_f32,) * 5,
        in_specs=[any_spec] * 9 + [pl.BlockSpec(memory_space=pltpu.SMEM)],
        out_specs=(any_spec,) * 6,
        scratch_shapes=[
            pltpu.VMEM((n_tok, width), BF16),
            pltpu.VMEM((1, width), F32),
            pltpu.VMEM((rows, cols), F32),
            pltpu.VMEM((rows, cols), F32),
            pltpu.VMEM((rows, cols), F32),
            pltpu.VMEM(momentum.shape, F32),
            pltpu.VMEM((n_tok, cols), BF16),
        ] + [pltpu.VMEM((rows, cols), F32)] * 5 + [
            pltpu.VMEM(frag_global.shape, F32),
            pltpu.VMEM(frag_local.shape, F32),
            pltpu.VMEM((n_tok, cols), BF16),
            pltpu.VMEM((n_tok, cols), BF16),
            pltpu.VMEM((rows, cols), BF16),
            pltpu.VMEM((SIDE, group, cols), BF16),
            pltpu.VMEM((SIDE, PLANES, n_tok, group), BF16),
            pltpu.VMEM((SIDE, n_tok, group), BF16),
            pltpu.VMEM((SIDE, group, cols), F32),
            pltpu.VMEM((SIDE, group, cols), BF16),
            pltpu.VMEM((2, 2, SIDE, rows, half), BF16),
            pltpu.VMEM((2, 2, SIDE, rows, cols), BF16),
            pltpu.VMEM((2, SIDE, rows, cols), F32),
            pltpu.VMEM((2, SIDE, rows, cols), BF16),
            pltpu.VMEM((2, 2, rows, half), BF16),
            pltpu.VMEM((2, 2, rows, cols), BF16),
            pltpu.VMEM((2, rows, cols), F32),
            pltpu.VMEM((2, rows, cols), BF16),
            pltpu.VMEM((2, rows, cols), BF16),
            pltpu.VMEM((n_tok, cols), F32),
            pltpu.VMEM((n_tok, cols), F32),
            pltpu.VMEM((n_tok, cols), F32),
            pltpu.VMEM((rows, cols), F32),
            pltpu.VMEM((2, rows // 2, cols // REPS), F32),
            pltpu.VMEM((2, rows, cols // REPS), F32),
            pltpu.VMEM((REPS, rows, cols // REPS), F32),
            pltpu.SemaphoreType.DMA((16,)),
            pltpu.SemaphoreType.DMA((6,)),
            pltpu.SemaphoreType.REGULAR,
            pltpu.SemaphoreType.DMA((N_SEMS,)),
            pltpu.SemaphoreType.DMA((N_SEMS,)),
        ],
        compiler_params=pltpu.CompilerParams(
            collective_id=0, has_side_effects=True, vmem_limit_bytes=60 * 1024 * 1024
        ),
        cost_estimate=pl.CostEstimate(flops=4 * n_tok * width * cols, bytes_accessed=10 * 1024 * 1024, transcendentals=0),
    )(tokens, gain, master, cot, frag_global, frag_local, moment, second, momentum, index)


def pass_kernel(*refs):
    n = (len(refs) - 2) // 3
    in_sem, out_sem = refs[-2:]
    reads = [pltpu.make_async_copy(refs[i], refs[2 * n + i], in_sem.at[i]) for i in range(n)]
    writes = [pltpu.make_async_copy(refs[2 * n + i], refs[n + i], out_sem.at[i]) for i in range(n)]
    for copy in reads:
        copy.start()
    for i in range(n):
        reads[i].wait()
        writes[i].start()
    for copy in writes:
        copy.wait()


def pass_on(arrays):
    any_spec = pl.BlockSpec(memory_space=pl.ANY)
    n = len(arrays)
    return pl.pallas_call(
        pass_kernel,
        out_shape=tuple(jax.ShapeDtypeStruct(a.shape, a.dtype) for a in arrays),
        in_specs=[any_spec] * n,
        out_specs=(any_spec,) * n,
        scratch_shapes=[pltpu.VMEM(a.shape, a.dtype) for a in arrays]
        + [pltpu.SemaphoreType.DMA((n,)), pltpu.SemaphoreType.DMA((n,))],
    )(*arrays)


def shards(
    tokens,
    norm_gain,
    master_weight,
    inner_moment,
    inner_second,
    cotangent,
    frag_global,
    frag_local,
    outer_momentum,
    fragment_index,
):
    key_rows, master_next, moment_next, second_next, new_global, new_outer = pass_on(exchange(
        tokens[0], norm_gain[None], master_weight[0], cotangent[0], frag_global, frag_local[0],
        inner_moment[0], inner_second[0], outer_momentum, fragment_index))
    return (
        key_rows[None],
        master_next[None],
        moment_next[None],
        second_next[None],
        new_global,
        new_outer,
    )


def solution(mesh):
    in_specs = (
        P("rep", "fsdp", None),
        P(),
        P("rep", "fsdp", None),
        P("rep", "fsdp", None),
        P("rep", "fsdp", None),
        P("rep", "fsdp", None),
        P(None, "fsdp", None),
        P("rep", None, "fsdp", None),
        P(None, "fsdp", None),
        P(),
    )
    out_specs = (
        P("rep", "fsdp", None),
        P("rep", "fsdp", None),
        P("rep", "fsdp", None),
        P("rep", "fsdp", None),
        P("fsdp", None),
        P("fsdp", None),
    )
    return jax.shard_map(shards, mesh=mesh, in_specs=in_specs, out_specs=out_specs, check_vma=False)
```

```python
import functools

import jax
import jax.numpy as jnp
from jax import lax
from jax.experimental import pallas as pl
from jax.experimental.pallas import tpu as pltpu
from jax.sharding import PartitionSpec as P

MESH = pl.DeviceIdType.MESH
F32 = jnp.float32
BF16 = jnp.bfloat16
REPS = 4
SIDE = 4
NFRAG = 2
PLANES = 2
STRIP = 32
N_SEMS = 192


def kernel(
    tokens_hbm, gain_hbm, master_hbm, cot_hbm, global_hbm, local_hbm, moment_hbm, second_hbm, momentum_hbm, index_ref,
    key_ref, master_ref, moment_ref, second_ref, global_ref, outer_ref,
    tok, gain, master, old_moment, old_second, momentum, key_v, master_v, moment_v, second_v, global_v, outer_v, frag_now, frag_local, cot, cot_oth,
    w_own, w, norm, norm_oth, part, part_bf, e_in, s_in, s_sum, s_bf, e2_in, s2_in,
    t_sum, t_bf, z_in, key_own, key_oth, key_in, diffs, re_in, rs_in, r_sum,
    in_sem, out_sem, here_sem, send_sem, recv_sem,
):
    rows, cols = master.shape
    n_tok = tok.shape[0]
    half = cols // 2
    lo, hi = pl.ds(0, half), pl.ds(half, half)
    group = norm.shape[-1]
    pair = PLANES * rows

    me = lax.axis_index("fsdp")
    rep = lax.axis_index("rep")
    core = me % 2
    x = (me // 2) % SIDE
    z = (me // (2 * SIDE)) % PLANES
    y = me // (2 * SIDE * PLANES)
    home = core == z

    def dev(y_, z_, x_, c_):
        return {"fsdp": ((y_ * PLANES + z_) * SIDE + x_) * 2 + c_}

    def along(axis, step):
        if axis == "x":
            return dev(y, z, (x + step + SIDE) % SIDE, core)
        return dev((y + step + SIDE) % SIDE, z, x, core)

    count = [0]
    started = []

    def slot():
        count[0] += 1
        return count[0] - 1

    def push(src, dst, to, sem=None, recv=None):
        sem = slot() if sem is None else sem
        copy = pltpu.make_async_remote_copy(
            src_ref=src,
            dst_ref=dst,
            send_sem=send_sem.at[sem],
            recv_sem=recv_sem.at[sem if recv is None else recv],
            device_id=to,
            device_id_type=MESH,
        )
        copy.start()
        return copy

    def send(src, dst, to):
        copy = push(src, dst, to)
        started.append(copy)
        return copy

    named = {}

    def remote(name, src, dst, to):
        if name not in named:
            named[name] = slot()
        return pltpu.make_async_remote_copy(
            src_ref=src, dst_ref=dst, send_sem=send_sem.at[named[name]], recv_sem=recv_sem.at[named[name]],
            device_id=to, device_id_type=MESH)

    loads = []

    def load(src, dst):
        copy = pltpu.make_async_copy(src, dst, in_sem.at[len(loads)])
        copy.start()
        loads.append(copy)
        return copy

    load_master = load(master_hbm, master)
    n_chunk = 4
    chunk = n_tok // n_chunk
    load_gain = load(gain_hbm, gain)
    load_tok = [load(tokens_hbm.at[pl.ds(i * chunk, chunk)], tok.at[pl.ds(i * chunk, chunk)]) for i in range(n_chunk)]
    load_cot = load(cot_hbm, cot)
    load_now = load(global_hbm, frag_now)
    load_loc = load(local_hbm, frag_local)
    load_rest = [load(moment_hbm, old_moment), load(second_hbm, old_second), load(momentum_hbm, momentum)]
    stores = []

    def store(src, dst):
        copy = pltpu.make_async_copy(src, dst, out_sem.at[len(stores)])
        copy.start()
        stores.append(copy)


    barrier = pltpu.get_barrier_semaphore()
    other_core = dev(y, z, x, 1 - core)
    peers = [along("x", 1), along("x", -1), along("y", 1), along("y", -1), other_core,
             dev(y, 1 - z, x, core), dev(y, 1 - z, x, 1 - core)]
    for peer in peers:
        pl.semaphore_signal(barrier, inc=1, device_id=peer, device_id_type=MESH)

    def rep_at(step):
        return {"rep": (rep + step + REPS) % REPS}

    STEP = (1, -1)
    for step in STEP:
        @pl.when(rep < (rep + step + REPS) % REPS)
        def _():
            pl.semaphore_signal(barrier, inc=1, device_id=rep_at(step), device_id_type=MESH)

    lower = (rep + 1) // 2

    load_master.wait()
    w_own[...] = master[...].astype(BF16)
    pl.semaphore_wait(barrier, len(peers) + lower)
    for step in STEP:
        @pl.when(rep > (rep + step + REPS) % REPS)
        def _():
            pl.semaphore_signal(here_sem, inc=1, device_id=rep_at(step), device_id_type=MESH)

    def w_rows(y_, x_, c_):
        return y_, pl.ds(pl.multiple_of(x_ * pair + c_ * rows, 16), rows)

    own_at = w.at[w_rows(y, x, core)]
    w_far, w_near = slot(), slot()
    w_got = (slot(), slot())
    far_copy = push(w_own, own_at, dev(y, 1 - z, x, z), w_far, w_got[0] + core)

    @pl.when(home)
    def _():
        w[w_rows(y, x, core)] = w_own[...]

    @pl.when(jnp.logical_not(home))
    def _():
        push(w_own, own_at, other_core, w_near, w_got[0] + core)

    tiles = group // 128
    n_group = norm.shape[0] * norm.shape[1]
    width = n_group * group

    def normalise(i):
        load_tok[i].wait()

        @pl.loop(0, chunk // STRIP)
        def _(s):
            at = pl.ds(pl.multiple_of(i * chunk + s * STRIP, STRIP), STRIP)
            total = jnp.zeros((STRIP, 128), F32)
            for t in range(width // 128):
                v = tok[at, t * 128:(t + 1) * 128].astype(F32)
                total = total + v * v
            mean = jnp.sum(total, axis=-1, keepdims=True) / width
            inverse = lax.rsqrt(mean + 1e-05)
            for t in range(width // 128):
                g, l = t // tiles, t % tiles
                v = tok[at, t * 128:(t + 1) * 128].astype(F32)
                v = v * inverse * gain[:, t * 128:(t + 1) * 128]
                norm[g // PLANES, g % PLANES, at, l * 128:(l + 1) * 128] = v.astype(BF16)

    def swap(i):
        at = pl.ds(i * chunk, chunk)
        return send(norm.at[:, 1 - core, at], norm_oth.at[:, at], other_core)

    first, second = ("x", "y"), ("y", "x")
    at1, at2 = (x, y), (y, x)

    def block(hf, a, b):
        y_, x_ = (b, a) if hf == 0 else (a, b)
        return w_rows(y_ % SIDE, x_ % SIDE, hf)

    def cut(where, columns):
        return (*where, columns)

    SIDE_COLS = (lo, hi)
    rel = (0, -1, 1, 2)
    FULL = (pl.ds(0, cols), lo)
    SIDES = ((lo, hi), (pl.ds(0, half // 2), pl.ds(half // 2, half // 2)))

    def piece_of(hf, i, j, columns):
        return w.at[cut(block(hf, at1[hf] + rel[i] + SIDE, at2[hf] + rel[j] + SIDE), columns)]

    def g1(role, hf, d):
        ref = piece_of(hf, 0, 0, FULL[role])
        return remote((1, hf, d), ref, ref, along(first[hf], STEP[d]))

    def g1f(role, hf, d):
        ref = piece_of(hf, 1 + d, 0, SIDES[role][d])
        return remote((2, hf, d), ref, ref, along(first[hf], STEP[d]))

    def g2(role, hf, i, d):
        ref = piece_of(hf, i, 0, FULL[role])
        return remote((3, hf, i, d), ref, ref, along(second[hf], STEP[d]))

    def g2f(role, hf, i, d):
        ref = piece_of(hf, i, 1 + d, SIDES[role][d])
        return remote((4, hf, i, d), ref, ref, along(second[hf], STEP[d]))

    def gz(hf, i, j):
        ref = piece_of(hf, i, j, hi)
        return remote((5, hf, i, j), ref, ref, dev(y, 1 - z, x, core))

    def each_role(step):
        @pl.when(home)
        def _():
            step(0)

        @pl.when(jnp.logical_not(home))
        def _():
            step(1)

    def gather_start(role):
        for hf in range(2):
            for d in range(2):
                g1(role, hf, d).start()
        for hf in range(2):
            for d in range(2):
                g2(role, hf, 0, d).start()

    def gather_first(role):
        for hf in range(2):
            for d in range(2):
                g1(role, hf, d).wait_recv()
                g1f(role, hf, d).start()
                for d2 in range(2):
                    g2(role, hf, 1 + d, d2).start()
                if role == 0:
                    gz(hf, 1 + d, 0).start()

    def gather_turn(role):
        for hf in range(2):
            gather_on(role, hf, 0)
            for d in range(2):
                g1f(role, hf, d).wait_recv()
            for d in range(2):
                g2(role, hf, 3, d).start()
            if role == 0:
                gz(hf, 3, 0).start()

    def gather_on(role, hf, i):
        for d in range(2):
            g2(role, hf, i, d).wait_recv()
            g2f(role, hf, i, d).start()
            if role == 0:
                gz(hf, i, 1 + d).start()

    def gather_last(role, i):
        for hf in range(2):
            for d in range(2):
                g2f(role, hf, i, d).wait_recv()
            if role == 0:
                gz(hf, i, 3).start()

    def gather_all(role, done):
        for hf in range(2):
            for d in range(2):
                getattr(g1(role, hf, d), done)()
                getattr(g1f(role, hf, d), done)()
                for i in range(SIDE):
                    getattr(g2(role, hf, i, d), done)()
                    getattr(g2f(role, hf, i, d), done)()

    def gather_far(done):
        for hf in range(2):
            for i in range(SIDE):
                for j in range(SIDE):
                    if i or j:
                        getattr(gz(hf, i, j), done)()

    def w_wait(c_):
        pltpu.make_async_remote_copy(
            src_ref=w_own, dst_ref=own_at, send_sem=send_sem.at[w_far], recv_sem=recv_sem.at[w_got[c_]],
            device_id=other_core, device_id_type=MESH).wait_recv()

    @pl.when(home)
    def _():
        for c_ in range(2):
            @pl.when(core != c_)
            def _():
                w_wait(c_)
        gather_start(0)

    load_cot.wait()
    cot_copy = send(cot, cot_oth, other_core)

    load_gain.wait()
    norm_copies = []
    for i in range(2):
        normalise(i)
        norm_copies.append(swap(i))

    @pl.when(jnp.logical_not(home))
    def _():
        for c_ in range(2):
            w_wait(c_)
        gather_start(1)

    for i in range(2, n_chunk):
        normalise(i)
        norm_copies.append(swap(i))

    load_now.wait()
    load_loc.wait()
    for copy in load_rest:
        copy.wait()
    odd = index_ref[...] % NFRAG == 1

    def picked(ref, *where):
        return jnp.where(odd, ref[(1, *where)], ref[(0, *where)])

    everything = pl.ds(0, rows), pl.ds(0, cols)
    diffs[...] = picked(frag_now, *everything) - picked(frag_local, *everything)
    quarter = cols // REPS
    ROWS = (pl.ds(0, rows // 2), pl.ds(rows // 2, rows // 2))

    def quarter_of(step, where):
        r = (rep + step + REPS) % REPS
        return where, pl.ds(pl.multiple_of(r * quarter, quarter), quarter)

    def r_e(d):
        return remote((6, d), diffs.at[quarter_of(2, ROWS[d])], re_in.at[d], rep_at(STEP[d]))

    def r_d(d):
        return remote((7, d), diffs.at[quarter_of(STEP[d], ROWS[1 - d])], rs_in.at[d, ROWS[1 - d]], rep_at(STEP[d]))

    def r_c(d):
        return remote((8, d), diffs.at[quarter_of(STEP[d], ROWS[d])], rs_in.at[d, ROWS[d]], rep_at(STEP[d]))

    def r_g(d):
        return remote((9, d), r_sum.at[rep], r_sum.at[rep], rep_at(STEP[d]))

    def r_f(d):
        ref = r_sum.at[(rep - STEP[d] + REPS) % REPS, ROWS[d]]
        return remote((10, d), ref, ref, rep_at(STEP[d]))

    def rep_start():
        @pl.when(lower < 2)
        def _():
            pl.semaphore_wait(here_sem, 2 - lower)

        for d in range(2):
            r_e(d).start()
        for d in range(2):
            r_d(d).start()

    def rep_combine():
        for d in range(2):
            r_e(d).wait_recv()
            where = quarter_of(STEP[d], ROWS[d])
            diffs[where] = diffs[where] + re_in[d]
            r_c(d).start()

    def rep_sum():
        for d in range(2):
            r_d(d).wait_recv()
            r_c(d).wait_recv()
        r_sum[rep] = diffs[quarter_of(0, pl.ds(0, rows))] + rs_in[0] + rs_in[1]
        for d in range(2):
            r_g(d).start()

    def rep_forward():
        for d in range(2):
            r_g(d).wait_recv()
            r_f(d).start()

    def rep_end():
        for d in range(2):
            r_f(d).wait_recv()
        round_count = (index_ref[...] // NFRAG).astype(F32)
        outer_rate = 0.7 * (1.0 - round_count / 512.0)
        for r in range(REPS):
            at = pl.ds(r * quarter, quarter)
            pseudo = r_sum[r] / REPS
            outer = 0.9 * picked(momentum, pl.ds(0, rows), at) + pseudo
            outer_v[:, at] = outer
            global_v[:, at] = picked(frag_now, pl.ds(0, rows), at) - outer_rate * (pseudo + 0.9 * outer)
        store(outer_v, outer_ref)
        store(global_v, global_ref)

    piece = group // 3
    over_tokens = (((0,), (0,)), ((), ()))

    @pl.loop(0, SIDE)
    def _(q):
        for j in range(3):
            part[q, j * piece:(j + 1) * piece, :] = lax.dot_general(
                norm[q, core, :, j * piece:(j + 1) * piece], cot[...], over_tokens, preferred_element_type=F32)

    each_role(gather_first)
    cot_copy.wait_recv()
    for copy in norm_copies:
        copy.wait_recv()

    @pl.loop(0, SIDE)
    def _(q):
        for j in range(3):
            total = part[q, j * piece:(j + 1) * piece, :] + lax.dot_general(
                norm_oth[q, :, j * piece:(j + 1) * piece], cot_oth[...], over_tokens, preferred_element_type=F32)
            part[q, j * piece:(j + 1) * piece, :] = total
            part_bf[q, j * piece:(j + 1) * piece, :] = total.astype(BF16)

    order = (3, 2, 1, 0)
    e_copies = [[None] * SIDE, [None] * SIDE]
    d_copies = [[None] * SIDE, [None] * SIDE]
    c_copies = [[None] * SIDE, [None] * SIDE]
    def spread(i):
        for hf in range(2):
            a = at1[hf] + rel[i] + SIDE
            e_copies[hf][i] = [
                send(part_bf.at[cut(block(hf, a, at2[hf] + 2), SIDE_COLS[d])], e_in.at[hf, d, i], along(second[hf], STEP[d]))
                for d in range(2)]

    def direct(i):
        for hf in range(2):
            a = at1[hf] + rel[i] + SIDE
            d_copies[hf][i] = [
                send(part_bf.at[cut(block(hf, a, at2[hf] + STEP[d] + SIDE), SIDE_COLS[1 - d])],
                     s_in.at[hf, d, i, :, SIDE_COLS[1 - d]], along(second[hf], STEP[d]))
                for d in range(2)]

    def combine(i):
        for hf in range(2):
            a = at1[hf] + rel[i] + SIDE
            copies = []
            for d in range(2):
                e_copies[hf][i][d].wait_recv()
                where = cut(block(hf, a, at2[hf] + STEP[d] + SIDE), SIDE_COLS[d])
                part_bf[where] = (part[where] + e_in[hf, d, i].astype(F32)).astype(BF16)
                copies.append(send(part_bf.at[where], s_in.at[hf, d, i, :, SIDE_COLS[d]], along(second[hf], STEP[d])))
            c_copies[hf][i] = copies

    e2_copies = [None, None]
    d2_copies = [[None, None], [None, None]]

    def settle(i):
        for hf in range(2):
            for d in range(2):
                d_copies[hf][i][d].wait_recv()
                c_copies[hf][i][d].wait_recv()
            a = at1[hf] + rel[i] + SIDE
            total = part[block(hf, a, at2[hf])] + s_in[hf, 0, i].astype(F32) + s_in[hf, 1, i].astype(F32)
            s_sum[hf, i] = total
            if i > 0:
                s_bf[hf, i] = total.astype(BF16)
            if i == 3:
                e2_copies[hf] = [
                    send(s_bf.at[hf, i, :, SIDE_COLS[d]], e2_in.at[hf, d], along(first[hf], STEP[d])) for d in range(2)]
            elif i > 0:
                d = 2 - i
                d2_copies[hf][d] = send(
                    s_bf.at[hf, i, :, SIDE_COLS[1 - d]], s2_in.at[hf, d, :, SIDE_COLS[1 - d]], along(first[hf], STEP[d]))

    c2_copies = [[None, None], [None, None]]

    def cross():
        for hf in range(2):
            for d in range(2):
                i = 2 - d
                e2_copies[hf][d].wait_recv()
                s_bf[hf, i, :, SIDE_COLS[d]] = (s_sum[hf, i, :, SIDE_COLS[d]] + e2_in[hf, d].astype(F32)).astype(BF16)
                c2_copies[hf][d] = send(
                    s_bf.at[hf, i, :, SIDE_COLS[d]], s2_in.at[hf, d, :, SIDE_COLS[d]], along(first[hf], STEP[d]))

    def on(i):
        each_role(lambda role: [gather_on(role, hf, i) for hf in range(2)])

    def last(i):
        each_role(lambda role: gather_last(role, i))

    rep_start()
    spread(3)
    spread(2)
    spread(1)
    spread(0)
    each_role(gather_turn)
    rep_combine()
    combine(3)
    direct(3)
    combine(2)
    direct(2)
    on(1)
    combine(1)
    on(2)
    direct(1)
    rep_sum()
    settle(3)
    on(3)
    combine(0)
    last(0)
    direct(0)
    rep_forward()
    last(1)
    settle(2)
    last(2)
    settle(1)
    cross()
    last(3)
    settle(0)
    for hf in range(2):
        for d in range(2):
            c2_copies[hf][d].wait_recv()
            d2_copies[hf][d].wait_recv()
        total = s_sum[hf, 0] + s2_in[hf, 0].astype(F32) + s2_in[hf, 1].astype(F32)
        t_sum[hf] = total
        t_bf[hf] = total.astype(BF16)

    z_near, z_far0, z_far1 = slot(), slot(), slot()
    z_got = (slot(), slot())

    @pl.when(home)
    def _():
        push(t_bf.at[1 - core], z_in.at[0], other_core, z_near, z_got[0])

    @pl.when(jnp.logical_not(home))
    def _():
        push(t_bf.at[0], z_in.at[1], dev(y, core, x, 0), z_far0, z_got[1])
        push(t_bf.at[1], z_in.at[1], dev(y, core, x, 1), z_far1, z_got[1])

    def in_last(hf, i, j):
        return (j if hf == 0 else i) == 3

    def far_wait(late):
        @pl.when(jnp.logical_not(home))
        def _():
            for hf in range(2):
                for i in range(SIDE):
                    for j in range(SIDE):
                        if (i or j) and in_last(hf, i, j) == late:
                            gz(hf, i, j).wait_recv()

    def key_terms(operand, steps):
        total = None
        for step in steps:
            q = (y + step) % SIDE
            term = jnp.dot(operand(q), w[q], preferred_element_type=F32)
            total = term if total is None else total + term
        return total

    far_wait(False)
    key_oth[...] = key_terms(lambda q: norm_oth[q], (0, 1, 3))
    key_own[...] = key_terms(lambda q: norm[q, core], (0, 1, 3))
    far_wait(True)
    key_copies = []
    half_rows = n_tok // 2
    for h in range(2):
        at = pl.ds(h * half_rows, half_rows)
        key_oth[at, :] = key_oth[at, :] + key_terms(lambda q: norm_oth[q, at], (2,))
        key_copies.append(send(key_oth.at[at], key_in.at[at], other_core))
    key_own[...] = key_own[...] + key_terms(lambda q: norm[q, core], (2,))
    rep_end()
    for h in range(2):
        at = pl.ds(h * half_rows, half_rows)
        key_copies[h].wait_recv()
        key_v[at, :] = (key_own[at, :] + key_in[at, :]).astype(BF16)
        store(key_v.at[at], key_ref.at[at])

    def z_copy(sem, got):
        return pltpu.make_async_remote_copy(
            src_ref=t_bf.at[0], dst_ref=z_in.at[0], send_sem=send_sem.at[sem], recv_sem=recv_sem.at[got],
            device_id=other_core, device_id_type=MESH)

    z_copy(z_far0, z_got[1]).wait_recv()

    def step_with(near):
        grad = near + z_in[1].astype(F32)
        old = master[...]
        moment_next = 0.9 * old_moment[...] + 0.1 * grad
        second_next = 0.95 * old_second[...] + 0.05 * grad * grad
        moment_v[...] = moment_next
        second_v[...] = second_next
        master_v[...] = old - 0.02 * (moment_next / (jnp.sqrt(second_next) + 1e-08) + 0.1 * old)

    @pl.when(home)
    def _():
        step_with(t_sum[core])

    @pl.when(jnp.logical_not(home))
    def _():
        z_copy(z_near, z_got[0]).wait_recv()
        step_with(z_in[0].astype(F32))

    store(master_v, master_ref)
    store(moment_v, moment_ref)
    store(second_v, second_ref)

    far_copy.wait_send()

    @pl.when(home)
    def _():
        z_copy(z_near, z_got[0]).wait_send()

    @pl.when(jnp.logical_not(home))
    def _():
        z_copy(w_near, z_got[0]).wait_send()
        z_copy(z_far0, z_got[0]).wait_send()
        z_copy(z_far1, z_got[0]).wait_send()

    each_role(lambda role: gather_all(role, "wait_send"))

    @pl.when(home)
    def _():
        gather_far("wait_send")

    for d in range(2):
        for copy in (r_e(d), r_d(d), r_c(d), r_g(d), r_f(d)):
            copy.wait_send()

    for copy in started:
        copy.wait_send()
    for copy in stores:
        copy.wait()


def exchange(tokens, gain, master, cot, frag_global, frag_local, moment, second, momentum, index):
    n_tok, width = tokens.shape
    rows, cols = master.shape
    n_group = SIDE * PLANES
    group = width // n_group
    half = cols // 2
    any_spec = pl.BlockSpec(memory_space=pl.ANY)
    rows_f32 = jax.ShapeDtypeStruct((rows, cols), F32)
    return pl.pallas_call(
        kernel,
        out_shape=(jax.ShapeDtypeStruct((n_tok, cols), BF16),) + (rows_f32,) * 5,
        in_specs=[any_spec] * 9 + [pl.BlockSpec(memory_space=pltpu.VMEM)],
        out_specs=(any_spec,) * 6,
        scratch_shapes=[
            pltpu.VMEM((n_tok, width), BF16),
            pltpu.VMEM((1, width), F32),
            pltpu.VMEM((rows, cols), F32),
            pltpu.VMEM((rows, cols), F32),
            pltpu.VMEM((rows, cols), F32),
            pltpu.VMEM(momentum.shape, F32),
            pltpu.VMEM((n_tok, cols), BF16),
        ] + [pltpu.VMEM((rows, cols), F32)] * 5 + [
            pltpu.VMEM(frag_global.shape, F32),
            pltpu.VMEM(frag_local.shape, F32),
            pltpu.VMEM((n_tok, cols), BF16),
            pltpu.VMEM((n_tok, cols), BF16),
            pltpu.VMEM((rows, cols), BF16),
            pltpu.VMEM((SIDE, group, cols), BF16),
            pltpu.VMEM((SIDE, PLANES, n_tok, group), BF16),
            pltpu.VMEM((SIDE, n_tok, group), BF16),
            pltpu.VMEM((SIDE, group, cols), F32),
            pltpu.VMEM((SIDE, group, cols), BF16),
            pltpu.VMEM((2, 2, SIDE, rows, half), BF16),
            pltpu.VMEM((2, 2, SIDE, rows, cols), BF16),
            pltpu.VMEM((2, SIDE, rows, cols), F32),
            pltpu.VMEM((2, SIDE, rows, cols), BF16),
            pltpu.VMEM((2, 2, rows, half), BF16),
            pltpu.VMEM((2, 2, rows, cols), BF16),
            pltpu.VMEM((2, rows, cols), F32),
            pltpu.VMEM((2, rows, cols), BF16),
            pltpu.VMEM((2, rows, cols), BF16),
            pltpu.VMEM((n_tok, cols), F32),
            pltpu.VMEM((n_tok, cols), F32),
            pltpu.VMEM((n_tok, cols), F32),
            pltpu.VMEM((rows, cols), F32),
            pltpu.VMEM((2, rows // 2, cols // REPS), F32),
            pltpu.VMEM((2, rows, cols // REPS), F32),
            pltpu.VMEM((REPS, rows, cols // REPS), F32),
            pltpu.SemaphoreType.DMA((16,)),
            pltpu.SemaphoreType.DMA((8,)),
            pltpu.SemaphoreType.REGULAR,
            pltpu.SemaphoreType.DMA((N_SEMS,)),
            pltpu.SemaphoreType.DMA((N_SEMS,)),
        ],
        compiler_params=pltpu.CompilerParams(
            collective_id=0, has_side_effects=True, vmem_limit_bytes=60 * 1024 * 1024
        ),
        cost_estimate=pl.CostEstimate(flops=4 * n_tok * width * cols, bytes_accessed=10 * 1024 * 1024, transcendentals=0),
    )(tokens, gain, master, cot, frag_global, frag_local, moment, second, momentum, index)


def pass_kernel(*refs):
    n = (len(refs) - 2) // 3
    in_sem, out_sem = refs[-2:]
    reads = [pltpu.make_async_copy(refs[i], refs[2 * n + i], in_sem.at[i]) for i in range(n)]
    writes = [pltpu.make_async_copy(refs[2 * n + i], refs[n + i], out_sem.at[i]) for i in range(n)]
    for copy in reads:
        copy.start()
    for i in range(n):
        reads[i].wait()
        writes[i].start()
    for copy in writes:
        copy.wait()


def pass_on(arrays):
    any_spec = pl.BlockSpec(memory_space=pl.ANY)
    n = len(arrays)
    return pl.pallas_call(
        pass_kernel,
        out_shape=tuple(jax.ShapeDtypeStruct(a.shape, a.dtype) for a in arrays),
        in_specs=[any_spec] * n,
        out_specs=(any_spec,) * n,
        scratch_shapes=[pltpu.VMEM(a.shape, a.dtype) for a in arrays]
        + [pltpu.SemaphoreType.DMA((n,)), pltpu.SemaphoreType.DMA((n,))],
    )(*arrays)


def shards(
    tokens,
    norm_gain,
    master_weight,
    inner_moment,
    inner_second,
    cotangent,
    frag_global,
    frag_local,
    outer_momentum,
    fragment_index,
):
    key_rows, master_next, moment_next, second_next, new_global, new_outer = pass_on(exchange(
        tokens[0], norm_gain[None], master_weight[0], cotangent[0], frag_global, frag_local[0],
        inner_moment[0], inner_second[0], outer_momentum, fragment_index[None]))
    return (
        key_rows[None],
        master_next[None],
        moment_next[None],
        second_next[None],
        new_global,
        new_outer,
    )


def solution(mesh):
    in_specs = (
        P("rep", "fsdp", None),
        P(),
        P("rep", "fsdp", None),
        P("rep", "fsdp", None),
        P("rep", "fsdp", None),
        P("rep", "fsdp", None),
        P(None, "fsdp", None),
        P("rep", None, "fsdp", None),
        P(None, "fsdp", None),
        P(),
    )
    out_specs = (
        P("rep", "fsdp", None),
        P("rep", "fsdp", None),
        P("rep", "fsdp", None),
        P("rep", "fsdp", None),
        P("fsdp", None),
        P("fsdp", None),
    )
    return jax.shard_map(shards, mesh=mesh, in_specs=in_specs, out_specs=out_specs, check_vma=False)
```

```python
import functools

import jax
import jax.numpy as jnp
from jax import lax
from jax.experimental import pallas as pl
from jax.experimental.pallas import tpu as pltpu
from jax.sharding import PartitionSpec as P

MESH = pl.DeviceIdType.MESH
F32 = jnp.float32
BF16 = jnp.bfloat16
REPS = 4
SIDE = 4
NFRAG = 2
PLANES = 2
STRIP = 32
N_SEMS = 192


def kernel(
    tokens_hbm, gain_hbm, master_hbm, cot_hbm, global_hbm, local_hbm, moment_hbm, second_hbm, momentum_hbm, index_ref,
    key_ref, master_ref, moment_ref, second_ref, global_ref, outer_ref,
    tok, gain, master, old_moment, old_second, momentum, key_v, master_v, moment_v, second_v, global_v, outer_v, frag_now, frag_local, cot, cot_oth,
    w_own, w, norm, norm_oth, part, part_bf, e_in, s_in, s_sum, s_bf, e2_in, s2_in,
    t_sum, t_bf, z_in, key_own, key_oth, key_in, diffs, re_in, rs_in, r_sum,
    in_sem, out_sem, here_sem, send_sem, recv_sem,
):
    rows, cols = master.shape
    n_tok = tok.shape[0]
    half = cols // 2
    lo, hi = pl.ds(0, half), pl.ds(half, half)
    group = norm.shape[-1]
    pair = PLANES * rows

    me = lax.axis_index("fsdp")
    rep = lax.axis_index("rep")
    core = me % 2
    x = (me // 2) % SIDE
    z = (me // (2 * SIDE)) % PLANES
    y = me // (2 * SIDE * PLANES)
    home = core == z

    def dev(y_, z_, x_, c_):
        return {"fsdp": ((y_ * PLANES + z_) * SIDE + x_) * 2 + c_}

    def along(axis, step):
        if axis == "x":
            return dev(y, z, (x + step + SIDE) % SIDE, core)
        return dev((y + step + SIDE) % SIDE, z, x, core)

    count = [0]
    started = []

    def slot():
        count[0] += 1
        return count[0] - 1

    def push(src, dst, to, sem=None, recv=None):
        sem = slot() if sem is None else sem
        copy = pltpu.make_async_remote_copy(
            src_ref=src,
            dst_ref=dst,
            send_sem=send_sem.at[sem],
            recv_sem=recv_sem.at[sem if recv is None else recv],
            device_id=to,
            device_id_type=MESH,
        )
        copy.start()
        return copy

    def send(src, dst, to):
        copy = push(src, dst, to)
        started.append(copy)
        return copy

    named = {}

    def remote(name, src, dst, to):
        if name not in named:
            named[name] = slot()
        return pltpu.make_async_remote_copy(
            src_ref=src, dst_ref=dst, send_sem=send_sem.at[named[name]], recv_sem=recv_sem.at[named[name]],
            device_id=to, device_id_type=MESH)

    loads = []

    def load(src, dst):
        copy = pltpu.make_async_copy(src, dst, in_sem.at[len(loads)])
        copy.start()
        loads.append(copy)
        return copy

    load_master = load(master_hbm, master)
    n_chunk = 4
    chunk = n_tok // n_chunk
    load_gain = load(gain_hbm, gain)
    load_tok = [load(tokens_hbm.at[pl.ds(i * chunk, chunk)], tok.at[pl.ds(i * chunk, chunk)]) for i in range(n_chunk)]
    load_cot = load(cot_hbm, cot)
    load_now = load(global_hbm, frag_now)
    load_loc = load(local_hbm, frag_local)
    load_rest = [load(moment_hbm, old_moment), load(second_hbm, old_second), load(momentum_hbm, momentum)]
    stores = []

    def store(src, dst):
        copy = pltpu.make_async_copy(src, dst, out_sem.at[len(stores)])
        copy.start()
        stores.append(copy)


    barrier = pltpu.get_barrier_semaphore()
    other_core = dev(y, z, x, 1 - core)
    peers = [along("x", 1), along("x", -1), along("y", 1), along("y", -1), other_core,
             dev(y, 1 - z, x, core), dev(y, 1 - z, x, 1 - core)]
    for peer in peers:
        pl.semaphore_signal(barrier, inc=1, device_id=peer, device_id_type=MESH)

    def rep_at(step):
        return {"rep": (rep + step + REPS) % REPS}

    STEP = (1, -1)
    for step in STEP:
        @pl.when(rep < (rep + step + REPS) % REPS)
        def _():
            pl.semaphore_signal(barrier, inc=1, device_id=rep_at(step), device_id_type=MESH)

    lower = (rep + 1) // 2

    load_master.wait()
    w_own[...] = master[...].astype(BF16)
    pl.semaphore_wait(barrier, len(peers) + lower)
    for step in STEP:
        @pl.when(rep > (rep + step + REPS) % REPS)
        def _():
            pl.semaphore_signal(here_sem, inc=1, device_id=rep_at(step), device_id_type=MESH)

    def w_rows(y_, x_, c_):
        return y_, pl.ds(pl.multiple_of(x_ * pair + c_ * rows, 16), rows)

    own_at = w.at[w_rows(y, x, core)]
    w_far, w_near = slot(), slot()
    w_got = (slot(), slot())
    w_far_hi = slot()
    w_got_hi = (slot(), slot())
    own_place = w_rows(y, x, core)
    far_copy = push(w_own.at[:, lo], w.at[(*own_place, lo)], dev(y, 1 - z, x, z), w_far, w_got[0] + core)
    far_copy_hi = push(w_own.at[:, hi], w.at[(*own_place, hi)], dev(y, 1 - z, x, z), w_far_hi, w_got_hi[0] + core)

    @pl.when(home)
    def _():
        w[w_rows(y, x, core)] = w_own[...]

    @pl.when(jnp.logical_not(home))
    def _():
        push(w_own, own_at, other_core, w_near, w_got[0] + core)

    tiles = group // 128
    n_group = norm.shape[0] * norm.shape[1]
    width = n_group * group

    def normalise(i):
        load_tok[i].wait()

        @pl.loop(0, chunk // STRIP)
        def _(s):
            at = pl.ds(pl.multiple_of(i * chunk + s * STRIP, STRIP), STRIP)
            total = jnp.zeros((STRIP, 128), F32)
            for t in range(width // 128):
                v = tok[at, t * 128:(t + 1) * 128].astype(F32)
                total = total + v * v
            mean = jnp.sum(total, axis=-1, keepdims=True) / width
            inverse = lax.rsqrt(mean + 1e-05)
            for t in range(width // 128):
                g, l = t // tiles, t % tiles
                v = tok[at, t * 128:(t + 1) * 128].astype(F32)
                v = v * inverse * gain[:, t * 128:(t + 1) * 128]
                norm[g // PLANES, g % PLANES, at, l * 128:(l + 1) * 128] = v.astype(BF16)

    def swap(i):
        at = pl.ds(i * chunk, chunk)
        return send(norm.at[:, 1 - core, at], norm_oth.at[:, at], other_core)

    first, second = ("x", "y"), ("y", "x")
    at1, at2 = (x, y), (y, x)

    def block(hf, a, b):
        y_, x_ = (b, a) if hf == 0 else (a, b)
        return w_rows(y_ % SIDE, x_ % SIDE, hf)

    def cut(where, columns):
        return (*where, columns)

    SIDE_COLS = (lo, hi)
    rel = (0, -1, 1, 2)
    FULL = (pl.ds(0, cols), lo)
    SIDES = ((lo, hi), (pl.ds(0, half // 2), pl.ds(half // 2, half // 2)))

    def piece_of(hf, i, j, columns):
        return w.at[cut(block(hf, at1[hf] + rel[i] + SIDE, at2[hf] + rel[j] + SIDE), columns)]

    def g1(role, hf, d):
        ref = piece_of(hf, 0, 0, FULL[role])
        return remote((1, hf, d), ref, ref, along(first[hf], STEP[d]))

    def g1f(role, hf, d):
        ref = piece_of(hf, 1 + d, 0, SIDES[role][d])
        return remote((2, hf, d), ref, ref, along(first[hf], STEP[d]))

    def g2(role, hf, i, d):
        ref = piece_of(hf, i, 0, FULL[role])
        return remote((3, hf, i, d), ref, ref, along(second[hf], STEP[d]))

    def g2f(role, hf, i, d):
        ref = piece_of(hf, i, 1 + d, SIDES[role][d])
        return remote((4, hf, i, d), ref, ref, along(second[hf], STEP[d]))

    def gz(hf, i, j):
        ref = piece_of(hf, i, j, hi)
        return remote((5, hf, i, j), ref, ref, dev(y, 1 - z, x, core))

    def each_role(step):
        @pl.when(home)
        def _():
            step(0)

        @pl.when(jnp.logical_not(home))
        def _():
            step(1)

    def gather_start(role):
        for hf in range(2):
            for d in range(2):
                g1(role, hf, d).start()
        for hf in range(2):
            for d in range(2):
                g2(role, hf, 0, d).start()

    def gather_first(role):
        for hf in range(2):
            for d in range(2):
                g1(role, hf, d).wait_recv()
                g1f(role, hf, d).start()
                for d2 in range(2):
                    g2(role, hf, 1 + d, d2).start()
                if role == 0:
                    gz(hf, 1 + d, 0).start()

    def gather_turn(role):
        for hf in range(2):
            gather_on(role, hf, 0)
            for d in range(2):
                g1f(role, hf, d).wait_recv()
            for d in range(2):
                g2(role, hf, 3, d).start()
            if role == 0:
                gz(hf, 3, 0).start()

    def gather_on(role, hf, i):
        for d in range(2):
            g2(role, hf, i, d).wait_recv()
            g2f(role, hf, i, d).start()
            if role == 0:
                gz(hf, i, 1 + d).start()

    def gather_last(role, i):
        for hf in range(2):
            for d in range(2):
                g2f(role, hf, i, d).wait_recv()
            if role == 0:
                gz(hf, i, 3).start()

    def gather_all(role, done):
        for hf in range(2):
            for d in range(2):
                getattr(g1(role, hf, d), done)()
                getattr(g1f(role, hf, d), done)()
                for i in range(SIDE):
                    getattr(g2(role, hf, i, d), done)()
                    getattr(g2f(role, hf, i, d), done)()

    def gather_far(done):
        for hf in range(2):
            for i in range(SIDE):
                for j in range(SIDE):
                    if i or j:
                        getattr(gz(hf, i, j), done)()

    def w_wait(got, src, dst):
        pltpu.make_async_remote_copy(
            src_ref=src, dst_ref=dst, send_sem=send_sem.at[w_far], recv_sem=recv_sem.at[got],
            device_id=other_core, device_id_type=MESH).wait_recv()

    @pl.when(home)
    def _():
        for c_ in range(2):
            @pl.when(core != c_)
            def _():
                w_wait(w_got[c_], w_own, own_at)
        gather_start(0)

    load_cot.wait()
    cot_copy = send(cot, cot_oth, other_core)

    load_gain.wait()
    norm_copies = []
    for i in range(2):
        normalise(i)
        norm_copies.append(swap(i))

    @pl.when(jnp.logical_not(home))
    def _():
        for c_ in range(2):
            w_wait(w_got[c_], w_own.at[:, lo], w.at[(*own_place, lo)])
        gather_start(1)

    for i in range(2, n_chunk):
        normalise(i)
        norm_copies.append(swap(i))

    load_now.wait()
    load_loc.wait()
    for copy in load_rest:
        copy.wait()
    odd = index_ref[...] % NFRAG == 1

    def picked(ref, *where):
        return jnp.where(odd, ref[(1, *where)], ref[(0, *where)])

    everything = pl.ds(0, rows), pl.ds(0, cols)
    diffs[...] = picked(frag_now, *everything) - picked(frag_local, *everything)
    quarter = cols // REPS
    ROWS = (pl.ds(0, rows // 2), pl.ds(rows // 2, rows // 2))

    def quarter_of(step, where):
        r = (rep + step + REPS) % REPS
        return where, pl.ds(pl.multiple_of(r * quarter, quarter), quarter)

    def r_e(d):
        return remote((6, d), diffs.at[quarter_of(2, ROWS[d])], re_in.at[d], rep_at(STEP[d]))

    def r_d(d):
        return remote((7, d), diffs.at[quarter_of(STEP[d], ROWS[1 - d])], rs_in.at[d, ROWS[1 - d]], rep_at(STEP[d]))

    def r_c(d):
        return remote((8, d), diffs.at[quarter_of(STEP[d], ROWS[d])], rs_in.at[d, ROWS[d]], rep_at(STEP[d]))

    def r_g(d):
        return remote((9, d), r_sum.at[rep], r_sum.at[rep], rep_at(STEP[d]))

    def r_f(d):
        ref = r_sum.at[(rep - STEP[d] + REPS) % REPS, ROWS[d]]
        return remote((10, d), ref, ref, rep_at(STEP[d]))

    def rep_start():
        @pl.when(lower < 2)
        def _():
            pl.semaphore_wait(here_sem, 2 - lower)

        for d in range(2):
            r_e(d).start()
        for d in range(2):
            r_d(d).start()

    def rep_combine():
        for d in range(2):
            r_e(d).wait_recv()
            where = quarter_of(STEP[d], ROWS[d])
            diffs[where] = diffs[where] + re_in[d]
            r_c(d).start()

    def rep_sum():
        for d in range(2):
            r_d(d).wait_recv()
            r_c(d).wait_recv()
        r_sum[rep] = diffs[quarter_of(0, pl.ds(0, rows))] + rs_in[0] + rs_in[1]
        for d in range(2):
            r_g(d).start()

    def rep_forward():
        for d in range(2):
            r_g(d).wait_recv()
            r_f(d).start()

    def rep_end():
        for d in range(2):
            r_f(d).wait_recv()
        round_count = (index_ref[...] // NFRAG).astype(F32)
        outer_rate = 0.7 * (1.0 - round_count / 512.0)
        for r in range(REPS):
            at = pl.ds(r * quarter, quarter)
            pseudo = r_sum[r] / REPS
            outer = 0.9 * picked(momentum, pl.ds(0, rows), at) + pseudo
            outer_v[:, at] = outer
            global_v[:, at] = picked(frag_now, pl.ds(0, rows), at) - outer_rate * (pseudo + 0.9 * outer)
        store(outer_v, outer_ref)
        store(global_v, global_ref)

    piece = group // 3
    over_tokens = (((0,), (0,)), ((), ()))

    @pl.loop(0, SIDE)
    def _(q):
        for j in range(3):
            part[q, j * piece:(j + 1) * piece, :] = lax.dot_general(
                norm[q, core, :, j * piece:(j + 1) * piece], cot[...], over_tokens, preferred_element_type=F32)

    each_role(gather_first)
    cot_copy.wait_recv()
    for copy in norm_copies:
        copy.wait_recv()

    @pl.loop(0, SIDE)
    def _(q):
        for j in range(3):
            total = part[q, j * piece:(j + 1) * piece, :] + lax.dot_general(
                norm_oth[q, :, j * piece:(j + 1) * piece], cot_oth[...], over_tokens, preferred_element_type=F32)
            part[q, j * piece:(j + 1) * piece, :] = total
            part_bf[q, j * piece:(j + 1) * piece, :] = total.astype(BF16)

    order = (3, 2, 1, 0)
    e_copies = [[None] * SIDE, [None] * SIDE]
    d_copies = [[None] * SIDE, [None] * SIDE]
    c_copies = [[None] * SIDE, [None] * SIDE]
    def spread(i):
        for hf in range(2):
            a = at1[hf] + rel[i] + SIDE
            e_copies[hf][i] = [
                send(part_bf.at[cut(block(hf, a, at2[hf] + 2), SIDE_COLS[d])], e_in.at[hf, d, i], along(second[hf], STEP[d]))
                for d in range(2)]

    def direct(i):
        for hf in range(2):
            a = at1[hf] + rel[i] + SIDE
            d_copies[hf][i] = [
                send(part_bf.at[cut(block(hf, a, at2[hf] + STEP[d] + SIDE), SIDE_COLS[1 - d])],
                     s_in.at[hf, d, i, :, SIDE_COLS[1 - d]], along(second[hf], STEP[d]))
                for d in range(2)]

    def combine(i):
        for hf in range(2):
            a = at1[hf] + rel[i] + SIDE
            copies = []
            for d in range(2):
                e_copies[hf][i][d].wait_recv()
                where = cut(block(hf, a, at2[hf] + STEP[d] + SIDE), SIDE_COLS[d])
                part_bf[where] = (part[where] + e_in[hf, d, i].astype(F32)).astype(BF16)
                copies.append(send(part_bf.at[where], s_in.at[hf, d, i, :, SIDE_COLS[d]], along(second[hf], STEP[d])))
            c_copies[hf][i] = copies

    e2_copies = [None, None]
    d2_copies = [[None, None], [None, None]]

    def settle(i):
        for hf in range(2):
            for d in range(2):
                d_copies[hf][i][d].wait_recv()
                c_copies[hf][i][d].wait_recv()
            a = at1[hf] + rel[i] + SIDE
            total = part[block(hf, a, at2[hf])] + s_in[hf, 0, i].astype(F32) + s_in[hf, 1, i].astype(F32)
            s_sum[hf, i] = total
            if i > 0:
                s_bf[hf, i] = total.astype(BF16)
            if i == 3:
                e2_copies[hf] = [
                    send(s_bf.at[hf, i, :, SIDE_COLS[d]], e2_in.at[hf, d], along(first[hf], STEP[d])) for d in range(2)]
            elif i > 0:
                d = 2 - i
                d2_copies[hf][d] = send(
                    s_bf.at[hf, i, :, SIDE_COLS[1 - d]], s2_in.at[hf, d, :, SIDE_COLS[1 - d]], along(first[hf], STEP[d]))

    c2_copies = [[None, None], [None, None]]

    def cross():
        for hf in range(2):
            for d in range(2):
                i = 2 - d
                e2_copies[hf][d].wait_recv()
                s_bf[hf, i, :, SIDE_COLS[d]] = (s_sum[hf, i, :, SIDE_COLS[d]] + e2_in[hf, d].astype(F32)).astype(BF16)
                c2_copies[hf][d] = send(
                    s_bf.at[hf, i, :, SIDE_COLS[d]], s2_in.at[hf, d, :, SIDE_COLS[d]], along(first[hf], STEP[d]))

    def on(i):
        each_role(lambda role: [gather_on(role, hf, i) for hf in range(2)])

    def last(i):
        each_role(lambda role: gather_last(role, i))

    rep_start()
    spread(3)
    spread(2)
    spread(1)
    spread(0)
    each_role(gather_turn)
    rep_combine()
    combine(3)
    direct(3)
    combine(2)
    direct(2)
    on(1)
    combine(1)
    on(2)
    direct(1)
    rep_sum()
    settle(3)
    on(3)
    combine(0)
    last(0)
    direct(0)
    rep_forward()
    last(1)
    settle(2)
    last(2)
    settle(1)
    cross()
    last(3)
    settle(0)
    for hf in range(2):
        for d in range(2):
            c2_copies[hf][d].wait_recv()
            d2_copies[hf][d].wait_recv()
        total = s_sum[hf, 0] + s2_in[hf, 0].astype(F32) + s2_in[hf, 1].astype(F32)
        t_sum[hf] = total
        t_bf[hf] = total.astype(BF16)

    z_near, z_far0, z_far1 = slot(), slot(), slot()
    z_got = (slot(), slot())

    @pl.when(home)
    def _():
        push(t_bf.at[1 - core], z_in.at[0], other_core, z_near, z_got[0])

    @pl.when(jnp.logical_not(home))
    def _():
        push(t_bf.at[0], z_in.at[1], dev(y, core, x, 0), z_far0, z_got[1])
        push(t_bf.at[1], z_in.at[1], dev(y, core, x, 1), z_far1, z_got[1])

    def in_last(hf, i, j):
        return (j if hf == 0 else i) == 3

    def far_wait(late):
        @pl.when(jnp.logical_not(home))
        def _():
            for hf in range(2):
                for i in range(SIDE):
                    for j in range(SIDE):
                        if (i or j) and in_last(hf, i, j) == late:
                            gz(hf, i, j).wait_recv()

    def key_terms(operand, steps):
        total = None
        for step in steps:
            q = (y + step) % SIDE
            term = jnp.dot(operand(q), w[q], preferred_element_type=F32)
            total = term if total is None else total + term
        return total

    @pl.when(jnp.logical_not(home))
    def _():
        for c_ in range(2):
            w_wait(w_got_hi[c_], w_own.at[:, hi], w.at[(*own_place, hi)])

    far_wait(False)
    key_oth[...] = key_terms(lambda q: norm_oth[q], (0, 1, 3))
    key_own[...] = key_terms(lambda q: norm[q, core], (0, 1, 3))
    far_wait(True)
    key_copies = []
    half_rows = n_tok // 2
    for h in range(2):
        at = pl.ds(h * half_rows, half_rows)
        key_oth[at, :] = key_oth[at, :] + key_terms(lambda q: norm_oth[q, at], (2,))
        key_copies.append(send(key_oth.at[at], key_in.at[at], other_core))
    key_own[...] = key_own[...] + key_terms(lambda q: norm[q, core], (2,))
    rep_end()
    for h in range(2):
        at = pl.ds(h * half_rows, half_rows)
        key_copies[h].wait_recv()
        key_v[at, :] = (key_own[at, :] + key_in[at, :]).astype(BF16)
        store(key_v.at[at], key_ref.at[at])

    def z_copy(sem, got):
        return pltpu.make_async_remote_copy(
            src_ref=t_bf.at[0], dst_ref=z_in.at[0], send_sem=send_sem.at[sem], recv_sem=recv_sem.at[got],
            device_id=other_core, device_id_type=MESH)

    z_copy(z_far0, z_got[1]).wait_recv()

    def step_with(near):
        grad = near + z_in[1].astype(F32)
        old = master[...]
        moment_next = 0.9 * old_moment[...] + 0.1 * grad
        second_next = 0.95 * old_second[...] + 0.05 * grad * grad
        moment_v[...] = moment_next
        second_v[...] = second_next
        master_v[...] = old - 0.02 * (moment_next / (jnp.sqrt(second_next) + 1e-08) + 0.1 * old)

    @pl.when(home)
    def _():
        step_with(t_sum[core])

    @pl.when(jnp.logical_not(home))
    def _():
        z_copy(z_near, z_got[0]).wait_recv()
        step_with(z_in[0].astype(F32))

    store(master_v, master_ref)
    store(moment_v, moment_ref)
    store(second_v, second_ref)

    far_copy.wait_send()
    far_copy_hi.wait_send()

    @pl.when(home)
    def _():
        z_copy(z_near, z_got[0]).wait_send()

    @pl.when(jnp.logical_not(home))
    def _():
        z_copy(w_near, z_got[0]).wait_send()
        z_copy(z_far0, z_got[0]).wait_send()
        z_copy(z_far1, z_got[0]).wait_send()

    each_role(lambda role: gather_all(role, "wait_send"))

    @pl.when(home)
    def _():
        gather_far("wait_send")

    for d in range(2):
        for copy in (r_e(d), r_d(d), r_c(d), r_g(d), r_f(d)):
            copy.wait_send()

    for copy in started:
        copy.wait_send()
    for copy in stores:
        copy.wait()


def exchange(tokens, gain, master, cot, frag_global, frag_local, moment, second, momentum, index):
    n_tok, width = tokens.shape
    rows, cols = master.shape
    n_group = SIDE * PLANES
    group = width // n_group
    half = cols // 2
    any_spec = pl.BlockSpec(memory_space=pl.ANY)
    rows_f32 = jax.ShapeDtypeStruct((rows, cols), F32)
    return pl.pallas_call(
        kernel,
        out_shape=(jax.ShapeDtypeStruct((n_tok, cols), BF16),) + (rows_f32,) * 5,
        in_specs=[any_spec] * 9 + [pl.BlockSpec(memory_space=pltpu.VMEM)],
        out_specs=(any_spec,) * 6,
        scratch_shapes=[
            pltpu.VMEM((n_tok, width), BF16),
            pltpu.VMEM((1, width), F32),
            pltpu.VMEM((rows, cols), F32),
            pltpu.VMEM((rows, cols), F32),
            pltpu.VMEM((rows, cols), F32),
            pltpu.VMEM(momentum.shape, F32),
            pltpu.VMEM((n_tok, cols), BF16),
        ] + [pltpu.VMEM((rows, cols), F32)] * 5 + [
            pltpu.VMEM(frag_global.shape, F32),
            pltpu.VMEM(frag_local.shape, F32),
            pltpu.VMEM((n_tok, cols), BF16),
            pltpu.VMEM((n_tok, cols), BF16),
            pltpu.VMEM((rows, cols), BF16),
            pltpu.VMEM((SIDE, group, cols), BF16),
            pltpu.VMEM((SIDE, PLANES, n_tok, group), BF16),
            pltpu.VMEM((SIDE, n_tok, group), BF16),
            pltpu.VMEM((SIDE, group, cols), F32),
            pltpu.VMEM((SIDE, group, cols), BF16),
            pltpu.VMEM((2, 2, SIDE, rows, half), BF16),
            pltpu.VMEM((2, 2, SIDE, rows, cols), BF16),
            pltpu.VMEM((2, SIDE, rows, cols), F32),
            pltpu.VMEM((2, SIDE, rows, cols), BF16),
            pltpu.VMEM((2, 2, rows, half), BF16),
            pltpu.VMEM((2, 2, rows, cols), BF16),
            pltpu.VMEM((2, rows, cols), F32),
            pltpu.VMEM((2, rows, cols), BF16),
            pltpu.VMEM((2, rows, cols), BF16),
            pltpu.VMEM((n_tok, cols), F32),
            pltpu.VMEM((n_tok, cols), F32),
            pltpu.VMEM((n_tok, cols), F32),
            pltpu.VMEM((rows, cols), F32),
            pltpu.VMEM((2, rows // 2, cols // REPS), F32),
            pltpu.VMEM((2, rows, cols // REPS), F32),
            pltpu.VMEM((REPS, rows, cols // REPS), F32),
            pltpu.SemaphoreType.DMA((16,)),
            pltpu.SemaphoreType.DMA((8,)),
            pltpu.SemaphoreType.REGULAR,
            pltpu.SemaphoreType.DMA((N_SEMS,)),
            pltpu.SemaphoreType.DMA((N_SEMS,)),
        ],
        compiler_params=pltpu.CompilerParams(
            collective_id=0, has_side_effects=True, vmem_limit_bytes=60 * 1024 * 1024
        ),
        cost_estimate=pl.CostEstimate(flops=4 * n_tok * width * cols, bytes_accessed=10 * 1024 * 1024, transcendentals=0),
    )(tokens, gain, master, cot, frag_global, frag_local, moment, second, momentum, index)


def pass_kernel(*refs):
    n = (len(refs) - 2) // 3
    in_sem, out_sem = refs[-2:]
    reads = [pltpu.make_async_copy(refs[i], refs[2 * n + i], in_sem.at[i]) for i in range(n)]
    writes = [pltpu.make_async_copy(refs[2 * n + i], refs[n + i], out_sem.at[i]) for i in range(n)]
    for copy in reads:
        copy.start()
    for i in range(n):
        reads[i].wait()
        writes[i].start()
    for copy in writes:
        copy.wait()


def pass_on(arrays):
    any_spec = pl.BlockSpec(memory_space=pl.ANY)
    n = len(arrays)
    return pl.pallas_call(
        pass_kernel,
        out_shape=tuple(jax.ShapeDtypeStruct(a.shape, a.dtype) for a in arrays),
        in_specs=[any_spec] * n,
        out_specs=(any_spec,) * n,
        scratch_shapes=[pltpu.VMEM(a.shape, a.dtype) for a in arrays]
        + [pltpu.SemaphoreType.DMA((n,)), pltpu.SemaphoreType.DMA((n,))],
    )(*arrays)


def shards(
    tokens,
    norm_gain,
    master_weight,
    inner_moment,
    inner_second,
    cotangent,
    frag_global,
    frag_local,
    outer_momentum,
    fragment_index,
):
    key_rows, master_next, moment_next, second_next, new_global, new_outer = pass_on(exchange(
        tokens[0], norm_gain[None], master_weight[0], cotangent[0], frag_global, frag_local[0],
        inner_moment[0], inner_second[0], outer_momentum, fragment_index[None]))
    return (
        key_rows[None],
        master_next[None],
        moment_next[None],
        second_next[None],
        new_global,
        new_outer,
    )


def solution(mesh):
    in_specs = (
        P("rep", "fsdp", None),
        P(),
        P("rep", "fsdp", None),
        P("rep", "fsdp", None),
        P("rep", "fsdp", None),
        P("rep", "fsdp", None),
        P(None, "fsdp", None),
        P("rep", None, "fsdp", None),
        P(None, "fsdp", None),
        P(),
    )
    out_specs = (
        P("rep", "fsdp", None),
        P("rep", "fsdp", None),
        P("rep", "fsdp", None),
        P("rep", "fsdp", None),
        P("fsdp", None),
        P("fsdp", None),
    )
    return jax.shard_map(shards, mesh=mesh, in_specs=in_specs, out_specs=out_specs, check_vma=False)
```

```python
import functools

import jax
import jax.numpy as jnp
from jax import lax
from jax.experimental import pallas as pl
from jax.experimental.pallas import tpu as pltpu
from jax.sharding import PartitionSpec as P

MESH = pl.DeviceIdType.MESH
F32 = jnp.float32
BF16 = jnp.bfloat16
REPS = 4
SIDE = 4
NFRAG = 2
PLANES = 2
STRIP = 32
N_SEMS = 192


def kernel(
    tokens_hbm, gain_hbm, master_hbm, cot_hbm, global_hbm, local_hbm, moment_hbm, second_hbm, momentum_hbm, index_ref,
    key_ref, master_ref, moment_ref, second_ref, global_ref, outer_ref,
    tok, gain, master, old_moment, old_second, momentum, key_v, master_v, moment_v, second_v, global_v, outer_v, frag_now, frag_local, cot, cot_oth,
    w_own, w, norm, norm_oth, part, part_bf, e_in, s_in, s_sum, s_bf, e2_in, s2_in,
    t_sum, t_bf, z_in, key_own, key_oth, key_in, diffs, re_in, rs_in, r_sum,
    in_sem, out_sem, here_sem, send_sem, recv_sem,
):
    rows, cols = master.shape
    n_tok = tok.shape[0]
    half = cols // 2
    lo, hi = pl.ds(0, half), pl.ds(half, half)
    group = norm.shape[-1]
    pair = PLANES * rows

    me = lax.axis_index("fsdp")
    rep = lax.axis_index("rep")
    core = me % 2
    x = (me // 2) % SIDE
    z = (me // (2 * SIDE)) % PLANES
    y = me // (2 * SIDE * PLANES)
    home = core == z

    def dev(y_, z_, x_, c_):
        return {"fsdp": ((y_ * PLANES + z_) * SIDE + x_) * 2 + c_}

    def along(axis, step):
        if axis == "x":
            return dev(y, z, (x + step + SIDE) % SIDE, core)
        return dev((y + step + SIDE) % SIDE, z, x, core)

    count = [0]
    started = []

    def slot():
        count[0] += 1
        return count[0] - 1

    def push(src, dst, to, sem=None, recv=None):
        sem = slot() if sem is None else sem
        copy = pltpu.make_async_remote_copy(
            src_ref=src,
            dst_ref=dst,
            send_sem=send_sem.at[sem],
            recv_sem=recv_sem.at[sem if recv is None else recv],
            device_id=to,
            device_id_type=MESH,
        )
        copy.start()
        return copy

    def send(src, dst, to):
        copy = push(src, dst, to)
        started.append(copy)
        return copy

    named = {}

    def remote(name, src, dst, to):
        if name not in named:
            named[name] = slot()
        return pltpu.make_async_remote_copy(
            src_ref=src, dst_ref=dst, send_sem=send_sem.at[named[name]], recv_sem=recv_sem.at[named[name]],
            device_id=to, device_id_type=MESH)

    loads = []

    def load(src, dst):
        copy = pltpu.make_async_copy(src, dst, in_sem.at[len(loads)])
        copy.start()
        loads.append(copy)
        return copy

    load_master = load(master_hbm, master)
    n_chunk = 4
    chunk = n_tok // n_chunk
    load_gain = load(gain_hbm, gain)
    load_tok = [load(tokens_hbm.at[pl.ds(i * chunk, chunk)], tok.at[pl.ds(i * chunk, chunk)]) for i in range(n_chunk)]
    load_cot = load(cot_hbm, cot)
    load_now = load(global_hbm, frag_now)
    load_loc = load(local_hbm, frag_local)
    load_rest = [load(moment_hbm, old_moment), load(second_hbm, old_second), load(momentum_hbm, momentum)]
    stores = []

    def store(src, dst):
        copy = pltpu.make_async_copy(src, dst, out_sem.at[len(stores)])
        copy.start()
        stores.append(copy)


    barrier = pltpu.get_barrier_semaphore()
    other_core = dev(y, z, x, 1 - core)
    peers = [along("x", 1), along("x", -1), along("y", 1), along("y", -1), other_core,
             dev(y, 1 - z, x, core), dev(y, 1 - z, x, 1 - core)]
    for peer in peers:
        pl.semaphore_signal(barrier, inc=1, device_id=peer, device_id_type=MESH)

    def rep_at(step):
        return {"rep": (rep + step + REPS) % REPS}

    STEP = (1, -1)
    for step in STEP:
        @pl.when(rep < (rep + step + REPS) % REPS)
        def _():
            pl.semaphore_signal(barrier, inc=1, device_id=rep_at(step), device_id_type=MESH)

    lower = (rep + 1) // 2

    load_master.wait()
    w_own[...] = master[...].astype(BF16)
    pl.semaphore_wait(barrier, len(peers) + lower)
    for step in STEP:
        @pl.when(rep > (rep + step + REPS) % REPS)
        def _():
            pl.semaphore_signal(here_sem, inc=1, device_id=rep_at(step), device_id_type=MESH)

    def w_rows(y_, x_, c_):
        return y_, pl.ds(pl.multiple_of(x_ * pair + c_ * rows, 16), rows)

    own_at = w.at[w_rows(y, x, core)]
    w_far, w_near = slot(), slot()
    w_got = (slot(), slot())
    @pl.when(home)
    def _():
        w[w_rows(y, x, core)] = w_own[...]

    @pl.when(jnp.logical_not(home))
    def _():
        push(w_own, own_at, other_core, w_near, w_got[0] + core)

    w_far_hi = slot()
    w_got_hi = (slot(), slot())
    own_place = w_rows(y, x, core)
    far_copy = push(w_own.at[:, lo], w.at[(*own_place, lo)], dev(y, 1 - z, x, z), w_far, w_got[0] + core)
    far_copy_hi = push(w_own.at[:, hi], w.at[(*own_place, hi)], dev(y, 1 - z, x, z), w_far_hi, w_got_hi[0] + core)

    tiles = group // 128
    n_group = norm.shape[0] * norm.shape[1]
    width = n_group * group

    def normalise(i):
        load_tok[i].wait()

        @pl.loop(0, chunk // STRIP)
        def _(s):
            at = pl.ds(pl.multiple_of(i * chunk + s * STRIP, STRIP), STRIP)
            total = jnp.zeros((STRIP, 128), F32)
            for t in range(width // 128):
                v = tok[at, t * 128:(t + 1) * 128].astype(F32)
                total = total + v * v
            mean = jnp.sum(total, axis=-1, keepdims=True) / width
            inverse = lax.rsqrt(mean + 1e-05)
            for t in range(width // 128):
                g, l = t // tiles, t % tiles
                v = tok[at, t * 128:(t + 1) * 128].astype(F32)
                v = v * inverse * gain[:, t * 128:(t + 1) * 128]
                norm[g // PLANES, g % PLANES, at, l * 128:(l + 1) * 128] = v.astype(BF16)

    def swap(i):
        at = pl.ds(i * chunk, chunk)
        return send(norm.at[:, 1 - core, at], norm_oth.at[:, at], other_core)

    first, second = ("x", "y"), ("y", "x")
    at1, at2 = (x, y), (y, x)

    def block(hf, a, b):
        y_, x_ = (b, a) if hf == 0 else (a, b)
        return w_rows(y_ % SIDE, x_ % SIDE, hf)

    def cut(where, columns):
        return (*where, columns)

    SIDE_COLS = (lo, hi)
    rel = (0, -1, 1, 2)
    FULL = (pl.ds(0, cols), lo)
    SIDES = ((lo, hi), (pl.ds(0, half // 2), pl.ds(half // 2, half // 2)))

    def piece_of(hf, i, j, columns):
        return w.at[cut(block(hf, at1[hf] + rel[i] + SIDE, at2[hf] + rel[j] + SIDE), columns)]

    def g1(role, hf, d):
        ref = piece_of(hf, 0, 0, FULL[role])
        return remote((1, hf, d), ref, ref, along(first[hf], STEP[d]))

    def g1f(role, hf, d):
        ref = piece_of(hf, 1 + d, 0, SIDES[role][d])
        return remote((2, hf, d), ref, ref, along(first[hf], STEP[d]))

    def g2(role, hf, i, d):
        ref = piece_of(hf, i, 0, FULL[role])
        return remote((3, hf, i, d), ref, ref, along(second[hf], STEP[d]))

    def g2f(role, hf, i, d):
        ref = piece_of(hf, i, 1 + d, SIDES[role][d])
        return remote((4, hf, i, d), ref, ref, along(second[hf], STEP[d]))

    def gz(hf, i, j):
        ref = piece_of(hf, i, j, hi)
        return remote((5, hf, i, j), ref, ref, dev(y, 1 - z, x, core))

    def each_role(step):
        @pl.when(home)
        def _():
            step(0)

        @pl.when(jnp.logical_not(home))
        def _():
            step(1)

    def gather_start(role, hf):
        for d in range(2):
            g1(role, hf, d).start()
        for d in range(2):
            g2(role, hf, 0, d).start()

    def gather_first(role):
        for hf in range(2):
            for d in range(2):
                g1(role, hf, d).wait_recv()
                g1f(role, hf, d).start()
                for d2 in range(2):
                    g2(role, hf, 1 + d, d2).start()
                if role == 0:
                    gz(hf, 1 + d, 0).start()

    def gather_turn(role):
        for hf in range(2):
            gather_on(role, hf, 0)
            for d in range(2):
                g1f(role, hf, d).wait_recv()
            for d in range(2):
                g2(role, hf, 3, d).start()
            if role == 0:
                gz(hf, 3, 0).start()

    def gather_on(role, hf, i):
        for d in range(2):
            g2(role, hf, i, d).wait_recv()
            g2f(role, hf, i, d).start()
            if role == 0:
                gz(hf, i, 1 + d).start()

    def gather_last(role, i):
        for hf in range(2):
            for d in range(2):
                g2f(role, hf, i, d).wait_recv()
            if role == 0:
                gz(hf, i, 3).start()

    def gather_all(role, done):
        for hf in range(2):
            for d in range(2):
                getattr(g1(role, hf, d), done)()
                getattr(g1f(role, hf, d), done)()
                for i in range(SIDE):
                    getattr(g2(role, hf, i, d), done)()
                    getattr(g2f(role, hf, i, d), done)()

    def gather_far(done):
        for hf in range(2):
            for i in range(SIDE):
                for j in range(SIDE):
                    if i or j:
                        getattr(gz(hf, i, j), done)()

    def w_wait(got, src, dst):
        pltpu.make_async_remote_copy(
            src_ref=src, dst_ref=dst, send_sem=send_sem.at[w_far], recv_sem=recv_sem.at[got],
            device_id=other_core, device_id_type=MESH).wait_recv()

    @pl.when(home)
    def _():
        for c_ in range(2):
            @pl.when(core == c_)
            def _():
                gather_start(0, c_)

        for c_ in range(2):
            @pl.when(core != c_)
            def _():
                w_wait(w_got[c_], w_own, own_at)
                gather_start(0, c_)

    load_cot.wait()
    cot_copy = send(cot, cot_oth, other_core)

    load_gain.wait()
    norm_copies = []
    for i in range(2):
        normalise(i)
        norm_copies.append(swap(i))

    @pl.when(jnp.logical_not(home))
    def _():
        for c_ in range(2):
            w_wait(w_got[c_], w_own.at[:, lo], w.at[(*own_place, lo)])
            gather_start(1, c_)

    for i in range(2, n_chunk):
        normalise(i)
        norm_copies.append(swap(i))

    load_now.wait()
    load_loc.wait()
    for copy in load_rest:
        copy.wait()
    odd = index_ref[...] % NFRAG == 1

    def picked(ref, *where):
        return jnp.where(odd, ref[(1, *where)], ref[(0, *where)])

    everything = pl.ds(0, rows), pl.ds(0, cols)
    diffs[...] = picked(frag_now, *everything) - picked(frag_local, *everything)
    quarter = cols // REPS
    ROWS = (pl.ds(0, rows // 2), pl.ds(rows // 2, rows // 2))

    def quarter_of(step, where):
        r = (rep + step + REPS) % REPS
        return where, pl.ds(pl.multiple_of(r * quarter, quarter), quarter)

    def r_e(d):
        return remote((6, d), diffs.at[quarter_of(2, ROWS[d])], re_in.at[d], rep_at(STEP[d]))

    def r_d(d):
        return remote((7, d), diffs.at[quarter_of(STEP[d], ROWS[1 - d])], rs_in.at[d, ROWS[1 - d]], rep_at(STEP[d]))

    def r_c(d):
        return remote((8, d), diffs.at[quarter_of(STEP[d], ROWS[d])], rs_in.at[d, ROWS[d]], rep_at(STEP[d]))

    def r_g(d):
        return remote((9, d), r_sum.at[rep], r_sum.at[rep], rep_at(STEP[d]))

    def r_f(d):
        ref = r_sum.at[(rep - STEP[d] + REPS) % REPS, ROWS[d]]
        return remote((10, d), ref, ref, rep_at(STEP[d]))

    def rep_start():
        @pl.when(lower < 2)
        def _():
            pl.semaphore_wait(here_sem, 2 - lower)

        for d in range(2):
            r_e(d).start()
        for d in range(2):
            r_d(d).start()

    def rep_combine():
        for d in range(2):
            r_e(d).wait_recv()
            where = quarter_of(STEP[d], ROWS[d])
            diffs[where] = diffs[where] + re_in[d]
            r_c(d).start()

    def rep_sum():
        for d in range(2):
            r_d(d).wait_recv()
            r_c(d).wait_recv()
        r_sum[rep] = diffs[quarter_of(0, pl.ds(0, rows))] + rs_in[0] + rs_in[1]
        for d in range(2):
            r_g(d).start()

    def rep_forward():
        for d in range(2):
            r_g(d).wait_recv()
            r_f(d).start()

    def rep_end():
        for d in range(2):
            r_f(d).wait_recv()
        round_count = (index_ref[...] // NFRAG).astype(F32)
        outer_rate = 0.7 * (1.0 - round_count / 512.0)
        for r in range(REPS):
            at = pl.ds(r * quarter, quarter)
            pseudo = r_sum[r] / REPS
            outer = 0.9 * picked(momentum, pl.ds(0, rows), at) + pseudo
            outer_v[:, at] = outer
            global_v[:, at] = picked(frag_now, pl.ds(0, rows), at) - outer_rate * (pseudo + 0.9 * outer)
        store(outer_v, outer_ref)
        store(global_v, global_ref)

    piece = group // 3
    over_tokens = (((0,), (0,)), ((), ()))

    @pl.loop(0, SIDE)
    def _(q):
        for j in range(3):
            part[q, j * piece:(j + 1) * piece, :] = lax.dot_general(
                norm[q, core, :, j * piece:(j + 1) * piece], cot[...], over_tokens, preferred_element_type=F32)

    each_role(gather_first)
    cot_copy.wait_recv()
    for copy in norm_copies:
        copy.wait_recv()

    @pl.loop(0, SIDE)
    def _(q):
        for j in range(3):
            total = part[q, j * piece:(j + 1) * piece, :] + lax.dot_general(
                norm_oth[q, :, j * piece:(j + 1) * piece], cot_oth[...], over_tokens, preferred_element_type=F32)
            part[q, j * piece:(j + 1) * piece, :] = total
            part_bf[q, j * piece:(j + 1) * piece, :] = total.astype(BF16)

    order = (3, 2, 1, 0)
    e_copies = [[None] * SIDE, [None] * SIDE]
    d_copies = [[None] * SIDE, [None] * SIDE]
    c_copies = [[None] * SIDE, [None] * SIDE]
    def spread(i):
        for hf in range(2):
            a = at1[hf] + rel[i] + SIDE
            e_copies[hf][i] = [
                send(part_bf.at[cut(block(hf, a, at2[hf] + 2), SIDE_COLS[d])], e_in.at[hf, d, i], along(second[hf], STEP[d]))
                for d in range(2)]

    def direct(i):
        for hf in range(2):
            a = at1[hf] + rel[i] + SIDE
            d_copies[hf][i] = [
                send(part_bf.at[cut(block(hf, a, at2[hf] + STEP[d] + SIDE), SIDE_COLS[1 - d])],
                     s_in.at[hf, d, i, :, SIDE_COLS[1 - d]], along(second[hf], STEP[d]))
                for d in range(2)]

    def combine(i):
        for hf in range(2):
            a = at1[hf] + rel[i] + SIDE
            copies = []
            for d in range(2):
                e_copies[hf][i][d].wait_recv()
                where = cut(block(hf, a, at2[hf] + STEP[d] + SIDE), SIDE_COLS[d])
                part_bf[where] = (part[where] + e_in[hf, d, i].astype(F32)).astype(BF16)
                copies.append(send(part_bf.at[where], s_in.at[hf, d, i, :, SIDE_COLS[d]], along(second[hf], STEP[d])))
            c_copies[hf][i] = copies

    e2_copies = [None, None]
    d2_copies = [[None, None], [None, None]]

    def settle(i):
        for hf in range(2):
            for d in range(2):
                d_copies[hf][i][d].wait_recv()
                c_copies[hf][i][d].wait_recv()
            a = at1[hf] + rel[i] + SIDE
            total = part[block(hf, a, at2[hf])] + s_in[hf, 0, i].astype(F32) + s_in[hf, 1, i].astype(F32)
            s_sum[hf, i] = total
            if i > 0:
                s_bf[hf, i] = total.astype(BF16)
            if i == 3:
                e2_copies[hf] = [
                    send(s_bf.at[hf, i, :, SIDE_COLS[d]], e2_in.at[hf, d], along(first[hf], STEP[d])) for d in range(2)]
            elif i > 0:
                d = 2 - i
                d2_copies[hf][d] = send(
                    s_bf.at[hf, i, :, SIDE_COLS[1 - d]], s2_in.at[hf, d, :, SIDE_COLS[1 - d]], along(first[hf], STEP[d]))

    c2_copies = [[None, None], [None, None]]

    def cross():
        for hf in range(2):
            for d in range(2):
                i = 2 - d
                e2_copies[hf][d].wait_recv()
                s_bf[hf, i, :, SIDE_COLS[d]] = (s_sum[hf, i, :, SIDE_COLS[d]] + e2_in[hf, d].astype(F32)).astype(BF16)
                c2_copies[hf][d] = send(
                    s_bf.at[hf, i, :, SIDE_COLS[d]], s2_in.at[hf, d, :, SIDE_COLS[d]], along(first[hf], STEP[d]))

    def on(i):
        each_role(lambda role: [gather_on(role, hf, i) for hf in range(2)])

    def last(i):
        each_role(lambda role: gather_last(role, i))

    rep_start()
    spread(3)
    spread(2)
    spread(1)
    spread(0)
    each_role(gather_turn)
    rep_combine()
    combine(3)
    direct(3)
    combine(2)
    direct(2)
    on(1)
    combine(1)
    on(2)
    direct(1)
    rep_sum()
    settle(3)
    on(3)
    combine(0)
    last(0)
    direct(0)
    rep_forward()
    last(1)
    settle(2)
    last(2)
    settle(1)
    cross()
    last(3)
    settle(0)
    for hf in range(2):
        for d in range(2):
            c2_copies[hf][d].wait_recv()
            d2_copies[hf][d].wait_recv()
        total = s_sum[hf, 0] + s2_in[hf, 0].astype(F32) + s2_in[hf, 1].astype(F32)
        t_sum[hf] = total
        t_bf[hf] = total.astype(BF16)

    z_near, z_far0, z_far1 = slot(), slot(), slot()
    z_got = (slot(), slot())

    @pl.when(home)
    def _():
        push(t_bf.at[1 - core], z_in.at[0], other_core, z_near, z_got[0])

    @pl.when(jnp.logical_not(home))
    def _():
        push(t_bf.at[0], z_in.at[1], dev(y, core, x, 0), z_far0, z_got[1])
        push(t_bf.at[1], z_in.at[1], dev(y, core, x, 1), z_far1, z_got[1])

    def in_last(hf, i, j):
        return (j if hf == 0 else i) == 3

    def far_wait(late):
        @pl.when(jnp.logical_not(home))
        def _():
            for hf in range(2):
                for i in range(SIDE):
                    for j in range(SIDE):
                        if (i or j) and in_last(hf, i, j) == late:
                            gz(hf, i, j).wait_recv()

    def key_terms(operand, steps):
        total = None
        for step in steps:
            q = (y + step) % SIDE
            term = jnp.dot(operand(q), w[q], preferred_element_type=F32)
            total = term if total is None else total + term
        return total

    @pl.when(jnp.logical_not(home))
    def _():
        for c_ in range(2):
            w_wait(w_got_hi[c_], w_own.at[:, hi], w.at[(*own_place, hi)])

    far_wait(False)
    key_oth[...] = key_terms(lambda q: norm_oth[q], (0, 1, 3))
    key_own[...] = key_terms(lambda q: norm[q, core], (0, 1, 3))
    far_wait(True)
    key_copies = []
    half_rows = n_tok // 2
    for h in range(2):
        at = pl.ds(h * half_rows, half_rows)
        key_oth[at, :] = key_oth[at, :] + key_terms(lambda q: norm_oth[q, at], (2,))
        key_copies.append(send(key_oth.at[at], key_in.at[at], other_core))
    key_own[...] = key_own[...] + key_terms(lambda q: norm[q, core], (2,))
    rep_end()
    for h in range(2):
        at = pl.ds(h * half_rows, half_rows)
        key_copies[h].wait_recv()
        key_v[at, :] = (key_own[at, :] + key_in[at, :]).astype(BF16)
        store(key_v.at[at], key_ref.at[at])

    def z_copy(sem, got):
        return pltpu.make_async_remote_copy(
            src_ref=t_bf.at[0], dst_ref=z_in.at[0], send_sem=send_sem.at[sem], recv_sem=recv_sem.at[got],
            device_id=other_core, device_id_type=MESH)

    z_copy(z_far0, z_got[1]).wait_recv()

    def step_with(near):
        grad = near + z_in[1].astype(F32)
        old = master[...]
        moment_next = 0.9 * old_moment[...] + 0.1 * grad
        second_next = 0.95 * old_second[...] + 0.05 * grad * grad
        moment_v[...] = moment_next
        second_v[...] = second_next
        master_v[...] = old - 0.02 * (moment_next / (jnp.sqrt(second_next) + 1e-08) + 0.1 * old)

    @pl.when(home)
    def _():
        step_with(t_sum[core])

    @pl.when(jnp.logical_not(home))
    def _():
        z_copy(z_near, z_got[0]).wait_recv()
        step_with(z_in[0].astype(F32))

    store(master_v, master_ref)
    store(moment_v, moment_ref)
    store(second_v, second_ref)

    far_copy.wait_send()
    far_copy_hi.wait_send()

    @pl.when(home)
    def _():
        z_copy(z_near, z_got[0]).wait_send()

    @pl.when(jnp.logical_not(home))
    def _():
        z_copy(w_near, z_got[0]).wait_send()
        z_copy(z_far0, z_got[0]).wait_send()
        z_copy(z_far1, z_got[0]).wait_send()

    each_role(lambda role: gather_all(role, "wait_send"))

    @pl.when(home)
    def _():
        gather_far("wait_send")

    for d in range(2):
        for copy in (r_e(d), r_d(d), r_c(d), r_g(d), r_f(d)):
            copy.wait_send()

    for copy in started:
        copy.wait_send()
    for copy in stores:
        copy.wait()


def exchange(tokens, gain, master, cot, frag_global, frag_local, moment, second, momentum, index):
    n_tok, width = tokens.shape
    rows, cols = master.shape
    n_group = SIDE * PLANES
    group = width // n_group
    half = cols // 2
    any_spec = pl.BlockSpec(memory_space=pl.ANY)
    rows_f32 = jax.ShapeDtypeStruct((rows, cols), F32)
    return pl.pallas_call(
        kernel,
        out_shape=(jax.ShapeDtypeStruct((n_tok, cols), BF16),) + (rows_f32,) * 5,
        in_specs=[any_spec] * 9 + [pl.BlockSpec(memory_space=pltpu.VMEM)],
        out_specs=(any_spec,) * 6,
        scratch_shapes=[
            pltpu.VMEM((n_tok, width), BF16),
            pltpu.VMEM((1, width), F32),
            pltpu.VMEM((rows, cols), F32),
            pltpu.VMEM((rows, cols), F32),
            pltpu.VMEM((rows, cols), F32),
            pltpu.VMEM(momentum.shape, F32),
            pltpu.VMEM((n_tok, cols), BF16),
        ] + [pltpu.VMEM((rows, cols), F32)] * 5 + [
            pltpu.VMEM(frag_global.shape, F32),
            pltpu.VMEM(frag_local.shape, F32),
            pltpu.VMEM((n_tok, cols), BF16),
            pltpu.VMEM((n_tok, cols), BF16),
            pltpu.VMEM((rows, cols), BF16),
            pltpu.VMEM((SIDE, group, cols), BF16),
            pltpu.VMEM((SIDE, PLANES, n_tok, group), BF16),
            pltpu.VMEM((SIDE, n_tok, group), BF16),
            pltpu.VMEM((SIDE, group, cols), F32),
            pltpu.VMEM((SIDE, group, cols), BF16),
            pltpu.VMEM((2, 2, SIDE, rows, half), BF16),
            pltpu.VMEM((2, 2, SIDE, rows, cols), BF16),
            pltpu.VMEM((2, SIDE, rows, cols), F32),
            pltpu.VMEM((2, SIDE, rows, cols), BF16),
            pltpu.VMEM((2, 2, rows, half), BF16),
            pltpu.VMEM((2, 2, rows, cols), BF16),
            pltpu.VMEM((2, rows, cols), F32),
            pltpu.VMEM((2, rows, cols), BF16),
            pltpu.VMEM((2, rows, cols), BF16),
            pltpu.VMEM((n_tok, cols), F32),
            pltpu.VMEM((n_tok, cols), F32),
            pltpu.VMEM((n_tok, cols), F32),
            pltpu.VMEM((rows, cols), F32),
            pltpu.VMEM((2, rows // 2, cols // REPS), F32),
            pltpu.VMEM((2, rows, cols // REPS), F32),
            pltpu.VMEM((REPS, rows, cols // REPS), F32),
            pltpu.SemaphoreType.DMA((16,)),
            pltpu.SemaphoreType.DMA((8,)),
            pltpu.SemaphoreType.REGULAR,
            pltpu.SemaphoreType.DMA((N_SEMS,)),
            pltpu.SemaphoreType.DMA((N_SEMS,)),
        ],
        compiler_params=pltpu.CompilerParams(
            collective_id=0, has_side_effects=True, vmem_limit_bytes=60 * 1024 * 1024
        ),
        cost_estimate=pl.CostEstimate(flops=4 * n_tok * width * cols, bytes_accessed=10 * 1024 * 1024, transcendentals=0),
    )(tokens, gain, master, cot, frag_global, frag_local, moment, second, momentum, index)


def pass_kernel(*refs):
    n = (len(refs) - 2) // 3
    in_sem, out_sem = refs[-2:]
    reads = [pltpu.make_async_copy(refs[i], refs[2 * n + i], in_sem.at[i]) for i in range(n)]
    writes = [pltpu.make_async_copy(refs[2 * n + i], refs[n + i], out_sem.at[i]) for i in range(n)]
    for copy in reads:
        copy.start()
    for i in range(n):
        reads[i].wait()
        writes[i].start()
    for copy in writes:
        copy.wait()


def pass_on(arrays):
    any_spec = pl.BlockSpec(memory_space=pl.ANY)
    n = len(arrays)
    return pl.pallas_call(
        pass_kernel,
        out_shape=tuple(jax.ShapeDtypeStruct(a.shape, a.dtype) for a in arrays),
        in_specs=[any_spec] * n,
        out_specs=(any_spec,) * n,
        scratch_shapes=[pltpu.VMEM(a.shape, a.dtype) for a in arrays]
        + [pltpu.SemaphoreType.DMA((n,)), pltpu.SemaphoreType.DMA((n,))],
    )(*arrays)


def shards(
    tokens,
    norm_gain,
    master_weight,
    inner_moment,
    inner_second,
    cotangent,
    frag_global,
    frag_local,
    outer_momentum,
    fragment_index,
):
    key_rows, master_next, moment_next, second_next, new_global, new_outer = pass_on(exchange(
        tokens[0], norm_gain[None], master_weight[0], cotangent[0], frag_global, frag_local[0],
        inner_moment[0], inner_second[0], outer_momentum, fragment_index[None]))
    return (
        key_rows[None],
        master_next[None],
        moment_next[None],
        second_next[None],
        new_global,
        new_outer,
    )


def solution(mesh):
    in_specs = (
        P("rep", "fsdp", None),
        P(),
        P("rep", "fsdp", None),
        P("rep", "fsdp", None),
        P("rep", "fsdp", None),
        P("rep", "fsdp", None),
        P(None, "fsdp", None),
        P("rep", None, "fsdp", None),
        P(None, "fsdp", None),
        P(),
    )
    out_specs = (
        P("rep", "fsdp", None),
        P("rep", "fsdp", None),
        P("rep", "fsdp", None),
        P("rep", "fsdp", None),
        P("fsdp", None),
        P("fsdp", None),
    )
    return jax.shard_map(shards, mesh=mesh, in_specs=in_specs, out_specs=out_specs, check_vma=False)
```
